128 devices in a mesh: cand: 8 (over x, core), tp: 16 (over z, y).
Axes of the slice: x: 4, y: 4, z: 4, core: 2. Of those that a mesh axis runs over, the one named last changes fastest.
Arguments:
- start_state: float32 [128], replicated, may hold values from -6 to 6
- goal: float32 [128], replicated, may hold values from -6 to 6
- mean_prev: float32 [128], replicated, may hold values from -0.5 to 0.5
- std_prev: float32 [128], replicated, may hold values from 0.1 to 0.5
- noise: float32 [1536, 128], P('cand'), may hold values from -23 to 23
- members: int32 [1536, 1], P('cand'), may hold values from 0 to 3; in each aligned block of 192 rows (0 to 191, 192 to 383, ...) at most 60 rows name the same one
- elites: int32 [192], replicated, may hold values from 0 to 1535, as said below
- w_in: bfloat16 [4, 144, 4096], P(None, None, 'tp'), may hold values from -0.5 to 0.5
- w_hid: bfloat16 [4, 4096, 4096], P(None, None, 'tp'), may hold values from -0.09375 to 0.09375
- w_out: bfloat16 [4, 4096, 128], P(None, 'tp'), may hold values from -0.09375 to 0.09375
Outputs:
- scores: float32 [1536], P('cand')
- new_mean: float32 [128], replicated
- new_std: float32 [128], replicated
The draws below stay inside these ranges and needn't reach their ends.
Inputs may be any that keep to these rules, and one draw needn't show every extreme that they name: `members`: among the candidates of one index of cand no member is named more than 60 times. `elites`: 192 distinct candidate numbers.
All inputs are finite; a program needn't handle non-finite values.
Results may differ from the reference program's by a relative error of at most 0.0085.
Values may be sent and summed in bfloat16 or wider, within the bound.
No kernel may reach another device: no remote copies, remote signals or barrier semaphores. Data moves between devices by JAX's collectives and lax.ppermute only.
A program may use at most 64 MiB of HBM per device.

```python
import math
import jax
import jax.numpy as jnp
import numpy as np
from jax import lax

H = 4096
S = 128
A = 16
HORIZON = 8
MEMBERS = 4
CAND_DEV = 192
CAP = 60
CANDS = 1536
ELITES = 192
N_CAND = 8


def draw_noise(key, part):
    first_key, second_key = jax.random.split(key)
    position = jnp.arange(CANDS, dtype=jnp.float32) / max(CANDS - 1, 1)
    factor = jnp.exp(jax.random.uniform(second_key, (CANDS,), jnp.float32, math.log(0.5), math.log(1.5)))
    growth = jnp.exp(position * math.log(3.0))
    sample = jnp.clip(jax.random.normal(first_key, (CANDS, HORIZON * A), jnp.float32), -5.0, 5.0)
    return (sample * (growth * factor)[:, None]).astype(jnp.float32)


def draw_elites(key, part):
    return jax.random.permutation(jax.random.fold_in(key, 7), CANDS)[:ELITES].astype(jnp.int32)


def block_levels(own_key, dims, cuts, smallest, high):
    def one(dim, blocks):
        draws = jax.random.uniform(jax.random.fold_in(jax.random.fold_in(own_key, 6), dim), (blocks,), jnp.float32, smallest / len(cuts), high / len(cuts))
        return jnp.repeat(jnp.exp(draws), dims[dim] // blocks).reshape((-1,) + (1,) * (len(dims) - dim - 1))

    loudness = one(*cuts[0])
    for cut in cuts[1:]:
        loudness = loudness * one(*cut)
    return loudness


def shared_out(own_key, own, number, rows, amount, top, most, skew):
    ranking = jax.random.permutation(own_key, amount)
    packed, common = shares(amount, rows * top, most, skew, True), shares(amount, rows * top, most, skew, False)
    places = jnp.arange(amount)

    def named(sizes, turn):
        used = int((sizes > 0).sum())
        fixed = max(1, used // 4)
        passed = fixed + (places - fixed + turn * (used - fixed)) % max(1, amount - fixed)
        return jnp.zeros((amount,), jnp.int32).at[ranking[jnp.where(places < fixed, places, passed)]].set(jnp.asarray(sizes, jnp.int32))

    sizes = jnp.where(number % 4 == 0, named(packed, number // 4), named(common, number - number // 4 - 1))
    mixed = jax.random.permutation(jax.random.fold_in(own, 3), amount)
    source_of, receiver = mixed[0:amount // 2 * 2:2], mixed[1:amount // 2 * 2:2]
    slack = jnp.minimum(sizes[source_of] - 1, most - sizes[receiver]) // 2
    slack = jnp.where((source_of == ranking[0]) | (receiver == ranking[0]) | (sizes[receiver] == 0), 0, jnp.maximum(slack, 0))
    passed = jax.random.randint(jax.random.fold_in(own, 4), (amount // 2,), 0, 1 << 20) % (slack + 1)
    sizes = sizes.at[source_of].add(-passed).at[receiver].add(passed)
    items = jnp.searchsorted(jnp.cumsum(sizes), jnp.arange(rows * top), side="right").astype(jnp.int32)
    grid = items.reshape(top, rows).T
    grid = grid[jax.random.permutation(jax.random.fold_in(own, 1), rows)]
    turn = jax.random.randint(jax.random.fold_in(own, 2), (rows, 1), 0, top)
    return jnp.take_along_axis(grid, (jnp.arange(top)[None, :] + turn) % top, axis=1)


def shares(number_of, total, limit, slope, full):
    loads = [(1 << 20) // math.isqrt(standing ** slope) + 1 for standing in range(1, number_of + 1)]
    largest = limit if full else min(limit, max(-(-total // number_of), total * loads[0] // sum(loads)))
    least = 1 if total - largest >= number_of - 1 else 0
    given, surplus = [largest] + [least] * (number_of - 1), total - largest - least * (number_of - 1)
    while surplus > 0:
        free = [i for i in range(1, number_of) if given[i] < largest] or [i for i in range(1, number_of) if given[i] < limit]
        pool, left = sum([loads[i] for i in free]), surplus
        for i in free:
            addition = min(limit - given[i], max(1, left * loads[i] // pool), surplus)
            given[i] = given[i] + addition
            surplus = surplus - addition
    return np.array(given)


def normal_values(rng, shape, width, most, shards=(), kind=jnp.bfloat16):
    factor_of = block_levels(rng, shape, shards, -0.22, 0.18) if shards else 1.0
    drawn = jax.random.normal(rng, shape, jnp.float32) * width * factor_of
    return jnp.minimum(jnp.maximum(drawn, -most), most).astype(kind)


def setup_inputs(seed: int = 0) -> dict:
    splits = jax.random.split(jax.random.key(seed), 11)
    start_state = normal_values(splits[0], (S,), 1.0, 6.0, (), jnp.float32)
    goal = normal_values(splits[1], (S,), 1.0, 6.0, (), jnp.float32)
    mean_prev = jnp.clip(jax.random.uniform(splits[2], (HORIZON * A,), jnp.float32, -0.5, 0.5), -0.5, 0.5)
    std_prev = jnp.clip(jnp.exp(jax.random.uniform(splits[3], (HORIZON * A,), jnp.float32, math.log(0.1), math.log(0.5))), 0.1, 0.5)
    noise = draw_noise(jax.random.fold_in(splits[10], 71), 0)
    members_keys = jax.random.split(jax.random.fold_in(splits[5], 1), CANDS // CAND_DEV)
    members_turns = jax.random.permutation(jax.random.fold_in(splits[5], 3), CANDS // CAND_DEV)
    members = jax.vmap(lambda own, number: shared_out(jax.random.fold_in(splits[5], 2), own, number, CAND_DEV, MEMBERS, 1, CAP, 1))(members_keys, members_turns).reshape((CANDS, 1))
    elites = draw_elites(jax.random.fold_in(splits[10], 71), 0)
    w_in = normal_values(splits[7], (MEMBERS, S + A, H), (S + A) ** -0.5, 0.5, ((2, 16),))
    w_hid = normal_values(splits[8], (MEMBERS, H, H), H ** -0.5, 0.09375, ((2, 16),))
    w_out = normal_values(splits[9], (MEMBERS, H, S), H ** -0.5, 0.09375, ((1, 16),))
    return {"start_state": start_state, "goal": goal, "mean_prev": mean_prev, "std_prev": std_prev, "noise": noise, "members": members, "elites": elites, "w_in": w_in, "w_hid": w_hid, "w_out": w_out}


def slot_matrix(member_block, member_count, capacity):
    onehot = (member_block[:, 0:1] == jnp.arange(member_count, dtype=jnp.int32)[None, :]).astype(jnp.float32)
    before = jnp.cumsum(onehot, axis=0) - onehot
    position = lax.optimization_barrier(jnp.sum(before * onehot, axis=1)).astype(jnp.int32)
    slot_number = member_block[:, 0].astype(jnp.int32) * capacity + position
    return (slot_number[None, :] == jnp.arange(member_count * capacity, dtype=jnp.int32)[:, None]).astype(jnp.float32)

def reward_of(states, goal, action):
    return -lax.optimization_barrier(jnp.mean((states - goal[None, :]) ** 2, axis=1)) - 0.1 * lax.optimization_barrier(jnp.mean(action * action, axis=1))

def reference(start_state, goal, mean_prev, std_prev, noise, members, elites, w_in, w_hid, w_out):
    actions = mean_prev[None, :] + std_prev[None, :] * noise

    def one_block(pair):
        block_actions, block_members = pair
        dispatch = slot_matrix(block_members, MEMBERS, CAP)
        slot_actions = jnp.dot(dispatch, block_actions, precision=lax.Precision.HIGHEST)
        slot_actions = slot_actions.reshape(MEMBERS, CAP, HORIZON, A)
        gathered = []
        for member in range(MEMBERS):
            states = jnp.zeros((CAP, S), jnp.float32) + start_state[None, :]
            running = jnp.zeros((CAP,), jnp.float32)
            for step_index in range(HORIZON):
                action = slot_actions[member, :, step_index, :]
                inputs = jnp.concatenate([states, action], axis=1).astype(jnp.bfloat16)
                hidden_one = jax.nn.silu(jnp.dot(inputs, w_in[member], preferred_element_type=jnp.float32)).astype(jnp.bfloat16)
                hidden_two = jax.nn.silu(jnp.dot(hidden_one, w_hid[member], preferred_element_type=jnp.float32)).astype(jnp.bfloat16)
                change = jnp.dot(hidden_two, w_out[member], preferred_element_type=jnp.float32)
                states = states + change
                running = running + reward_of(states, goal, action)
            gathered.append(running)
        slot_returns = jnp.concatenate(gathered)
        return jnp.dot(slot_returns, dispatch, precision=lax.Precision.HIGHEST)
    returns = lax.map(one_block, (actions.reshape(N_CAND, CAND_DEV, HORIZON * A), members.reshape(N_CAND, CAND_DEV, 1)))
    returns = returns.reshape(CANDS)
    return_mean = jnp.sum(returns) / CANDS
    return_var = jnp.sum((returns - return_mean) ** 2) / CANDS
    scores = (returns - return_mean) / jnp.sqrt(return_var + 1e-06)
    chosen = jnp.zeros((CANDS,), jnp.float32).at[elites].set(1.0)
    weights = chosen * (0.5 + jax.nn.sigmoid(scores))
    weight_sum = jnp.sum(weights)
    new_mean = jnp.dot(weights, actions, precision=lax.Precision.HIGHEST) / weight_sum
    new_var = jnp.dot(weights, (actions - new_mean[None, :]) ** 2, precision=lax.Precision.HIGHEST) / weight_sum
    new_std = jnp.sqrt(new_var + 1e-06)
    return (scores, new_mean, new_std)
```

```python
import functools
import jax
import jax.numpy as jnp
from jax import lax
from jax.experimental import pallas as pl
from jax.experimental.pallas import tpu as pltpu
from jax.sharding import Mesh, PartitionSpec as P

HORIZON = 8
RING = 4
CORES = 2
UNITS = 128


def silu(v):
    return (0.5 * v) * (1.0 + jnp.tanh(0.5 * v))


def shift(value, first, by):
    pairs = []
    for core in range(CORES):
        for z in range(RING):
            for y in range(RING):
                along_y = (core == 0) == first
                to = (z, (y + by) % RING) if along_y else ((z + by) % RING, y)
                pairs.append(((core * RING + z) * RING + y, (core * RING + to[0]) * RING + to[1]))
    return lax.ppermute(value, ("core", "z", "y"), pairs)


def gathered_round(value, first):
    half = value.shape[0] // 2
    left = shift(value, first, 1)
    right = shift(value, first, -1)
    far_low = shift(left[:half], first, 1)
    far_high = shift(right[half:], first, -1)
    return [value, left, right, far_low, far_high]


def step_kernel(first, last, *refs):
    if first:
        state_ref, action_ref, goal_ref, win_ref = refs[:4]
        weight_refs = refs[4:-2]
        state_out, partial_out = refs[-2:]
        state = jnp.broadcast_to(state_ref[...], state_out.shape)
        state_out[...] = state
    else:
        state_ref, own_ref, other_ref, reward_ref, before_ref, action_ref, goal_ref, win_ref = refs[:8]
        weight_refs = refs[8:-3]
        state_out, reward_out, partial_out = refs[-3:]
        state = state_ref[...] + (own_ref[...] + other_ref[...])
        before = before_ref[...]
        miss = state - goal_ref[...]
        reward = -jnp.mean(miss * miss, axis=1, keepdims=True) - 0.1 * jnp.mean(
            before * before, axis=1, keepdims=True
        )
        reward_out[...] = reward_ref[...] + reward
        state_out[...] = state
    inputs = jnp.concatenate([state, action_ref[...]], axis=1).astype(jnp.bfloat16)
    hidden = win_ref.shape[1]
    pieces = []
    wide = 1024
    for at in range(0, hidden, wide):
        pre = jnp.dot(inputs, win_ref[:, at : at + wide], preferred_element_type=jnp.float32)
        pieces.append(silu(pre).astype(jnp.bfloat16))
    hidden_one = jnp.concatenate(pieces, axis=1)
    block = hidden + UNITS
    total = jnp.zeros(partial_out.shape, jnp.float32)
    for ref in weight_refs:
        for pair in range(ref.shape[0] // (2 * block)):
            a, b = 2 * pair * block, (2 * pair + 1) * block
            weight = jnp.concatenate([ref[a : a + hidden, :], ref[b : b + hidden, :]], axis=1)
            pre = jnp.dot(hidden_one, weight, preferred_element_type=jnp.float32)
            hidden_two = silu(pre).astype(jnp.bfloat16)
            out = jnp.concatenate([ref[a + hidden : a + block, :], ref[b + hidden : b + block, :]], axis=0)
            total = total + jnp.dot(hidden_two, out, preferred_element_type=jnp.float32)
    partial_out[...] = total


def step(state, own, other, reward, before, action, goal, w_in, weights):
    rows = action.shape[0]
    first = own is None
    width = goal.shape[1]
    shape = jax.ShapeDtypeStruct((rows, width), jnp.float32)
    if first:
        args = (state, action, goal, w_in, *weights)
        outs = (shape, shape)
    else:
        args = (state, own, other, reward, before, action, goal, w_in, *weights)
        outs = (shape, jax.ShapeDtypeStruct((rows, 1), jnp.float32), shape)
    return pl.pallas_call(
        functools.partial(step_kernel, first, False),
        out_shape=outs,
        in_specs=[pl.BlockSpec(memory_space=pltpu.VMEM)] * len(args),
        out_specs=tuple([pl.BlockSpec(memory_space=pltpu.VMEM)] * len(outs)),
        compiler_params=pltpu.CompilerParams(vmem_limit_bytes=56 * 1024 * 1024),
    )(*args)


def report_kernel(state_ref, own_ref, other_ref, reward_ref, before_ref, goal_ref, flags_ref, out_ref):
    state = state_ref[...] + (own_ref[...] + other_ref[...])
    before = before_ref[...]
    miss = state - goal_ref[...]
    reward = -jnp.mean(miss * miss, axis=1, keepdims=True) - 0.1 * jnp.mean(before * before, axis=1, keepdims=True)
    returns = reward_ref[...] + reward
    flags = flags_ref[...]
    rows = returns.shape[0]
    lane = lax.broadcasted_iota(jnp.int32, (rows, 128), 1)
    row = lax.broadcasted_iota(jnp.int32, (rows, 128), 0)
    valid = flags[:, 0:1]
    spread = (
        jnp.where(lane == row, valid * returns, 0.0)
        + jnp.where(lane == row + rows, valid, 0.0)
        + jnp.where(lane == row + 2 * rows, flags[:, 1:2], 0.0)
    )
    message = jnp.sum(spread, axis=0, keepdims=True)
    out_ref[...] = jnp.broadcast_to(message[None], out_ref.shape)


def finish_kernel(at_ref, message_ref, actions_ref, dispatch_ref, scores_ref, mean_ref, std_ref):
    rows = 32
    count = 1536.0
    message = message_ref[...]
    returns = message[:, 0:rows]
    valid = message[:, rows : 2 * rows]
    elite = message[:, 2 * rows : 3 * rows]
    return_mean = jnp.sum(returns, keepdims=True) / count
    off = (returns - return_mean) * valid
    return_var = jnp.sum(off * off, keepdims=True) / count
    deviation = jnp.sqrt(return_var + 1e-06)
    scores = off / deviation
    weights = elite * (0.5 + jax.nn.sigmoid(scores))
    at = at_ref[0]
    lane = lax.broadcasted_iota(jnp.int32, scores.shape, 1)
    own = jnp.zeros(scores_ref.shape, jnp.float32)
    slots = scores.shape[0]
    for j in range(4):
        column = jnp.sum(jnp.where(lane == at * 4 + j, scores, 0.0), axis=1, keepdims=True)
        own = own + jnp.sum(column * dispatch_ref[j * slots : (j + 1) * slots, :], axis=0, keepdims=True)
    scores_ref[...] = own
    weight_sum = jnp.sum(weights, keepdims=True)
    total = jnp.zeros(actions_ref.shape[1:], jnp.float32)
    for l in range(rows):
        total = total + weights[:, l : l + 1] * actions_ref[l]
    mean = jnp.sum(total, axis=0, keepdims=True) / weight_sum
    total = jnp.zeros(actions_ref.shape[1:], jnp.float32)
    for l in range(rows):
        away = actions_ref[l] - mean
        total = total + weights[:, l : l + 1] * (away * away)
    var = jnp.sum(total, axis=0, keepdims=True) / weight_sum
    mean_ref[...] = mean
    std_ref[...] = jnp.sqrt(var + 1e-06)


def on_device(start_state, goal, mean_prev, std_prev, noise, members, elites, w_in, w_hid, w_out):
    local_count = noise.shape[0]
    member_count, hidden = w_hid.shape[0], w_hid.shape[1]
    width = start_state.shape[0]
    action_width = mean_prev.shape[0] // HORIZON
    member = lax.axis_index("x")
    core = lax.axis_index("core")
    place = lax.axis_index("z") * RING + lax.axis_index("y")
    places = RING * RING
    each = 4

    own_hid = lax.dynamic_slice(w_hid, (member, 0, core * UNITS), (1, hidden, UNITS))[0]
    own_out = lax.dynamic_slice(w_out, (member, core * UNITS, 0), (1, UNITS, width))[0]
    mine = jnp.concatenate([own_hid, own_out], axis=0)
    row_of_chips = jnp.concatenate(gathered_round(mine, True), axis=0)
    weights = gathered_round(row_of_chips, False)
    own_in = lax.dynamic_index_in_dim(w_in, member, 0, False)
    input_layer = lax.all_gather(own_in, ("z", "y"), axis=1, tiled=True)

    actions = mean_prev[None, :] + std_prev[None, :] * noise
    onehot = (members == jnp.arange(member_count, dtype=jnp.int32)[None, :]).astype(jnp.float32)
    before = jnp.cumsum(onehot, axis=0) - onehot
    position = jnp.sum(before * onehot, axis=1).astype(jnp.int32)
    slot = (position % each) * (member_count * places) + members[:, 0] * places + position // each
    slot_count = each * member_count * places
    dispatch = (slot[None, :] == jnp.arange(slot_count, dtype=jnp.int32)[:, None]).astype(jnp.float32)
    first_index = (member * CORES + core) * local_count
    numbers = first_index + jnp.arange(local_count, dtype=jnp.int32)
    chosen = jnp.sum((elites[:, None] == numbers[None, :]).astype(jnp.float32), axis=0)
    flags = jnp.stack([jnp.ones_like(chosen), chosen], axis=1)
    flags = jnp.concatenate([flags, jnp.zeros((local_count, 126), jnp.float32)], axis=1)
    table = jnp.concatenate([actions, flags], axis=1)
    slot_table = jnp.dot(dispatch, table, precision=lax.Precision.HIGHEST)
    slot_actions = slot_table[:, : actions.shape[1]].reshape(each, member_count * places, -1)
    all_actions = lax.all_gather(slot_actions, ("core", "x"), axis=0, tiled=True)

    to_send = lax.dynamic_index_in_dim(
        slot_table.reshape(each, member_count, places, -1), place, 2, False
    ).transpose(1, 0, 2)
    received = lax.all_to_all(to_send, "x", 0, 0, tiled=True).reshape(RING * each, -1)
    opposite = lax.ppermute(received, "core", [(0, 1), (1, 0)])
    low = jnp.where(core == 0, received, opposite)
    high = jnp.where(core == 0, opposite, received)
    rows = jnp.concatenate([low, high], axis=0)
    row_flags = rows[:, actions.shape[1] :]
    action_of = [rows[:, t * action_width : (t + 1) * action_width] for t in range(HORIZON)]

    goal_row = goal[None, :]
    state, partial = step(start_state[None, :], None, None, None, None, action_of[0], goal_row, input_layer, weights)
    reward = jnp.zeros((rows.shape[0], 1), jnp.float32)
    for t in range(1, HORIZON):
        other = lax.ppermute(partial, "core", [(0, 1), (1, 0)])
        state, reward, partial = step(
            state, partial, other, reward, action_of[t - 1], action_of[t], goal_row, input_layer, weights
        )
    other = lax.ppermute(partial, "core", [(0, 1), (1, 0)])
    vmem = pl.BlockSpec(memory_space=pltpu.VMEM)
    chips = RING * places
    report = pl.pallas_call(
        report_kernel,
        out_shape=jax.ShapeDtypeStruct((chips, 1, 128), jnp.float32),
        in_specs=[vmem] * 7,
        out_specs=vmem,
    )(state, partial, other, reward, action_of[HORIZON - 1], goal_row, row_flags)
    messages = lax.all_to_all(report, ("x", "z", "y"), 0, 0, tiled=True).reshape(chips, 128)
    at = (core * RING + member).astype(jnp.int32).reshape(1)
    scores, new_mean, new_std = pl.pallas_call(
        finish_kernel,
        out_shape=(
            jax.ShapeDtypeStruct((1, local_count), jnp.float32),
            jax.ShapeDtypeStruct((1, width), jnp.float32),
            jax.ShapeDtypeStruct((1, width), jnp.float32),
        ),
        in_specs=[pl.BlockSpec(memory_space=pltpu.SMEM), vmem, vmem, vmem],
        out_specs=(vmem, vmem, vmem),
    )(at, messages, all_actions, dispatch)
    return (scores.reshape(local_count), new_mean.reshape(width), new_std.reshape(width))


def solution(mesh):
    chips = Mesh(mesh.devices.reshape(RING, CORES, RING, RING), ("x", "core", "z", "y"))
    cand, tp = ("x", "core"), ("z", "y")
    placed = (
        P(),
        P(),
        P(),
        P(),
        P(cand, None),
        P(cand, None),
        P(),
        P(None, None, tp),
        P(None, None, tp),
        P(None, tp, None),
    )
    return jax.shard_map(
        on_device, mesh=chips, in_specs=placed, out_specs=(P(cand), P(), P()), check_vma=False
    )
```

```python
import functools
import jax
import jax.numpy as jnp
from jax import lax
from jax.experimental import pallas as pl
from jax.experimental.pallas import tpu as pltpu
from jax.sharding import Mesh, PartitionSpec as P

HORIZON = 8
RING = 4
CORES = 2


def silu(v):
    return (0.5 * v) * (1.0 + jnp.tanh(0.5 * v))


def shift(value, own_axis, by):
    pairs = []
    for core in range(CORES):
        for z in range(RING):
            for y in range(RING):
                along_y = (core == 0) == own_axis
                to = (z, (y + by) % RING) if along_y else ((z + by) % RING, y)
                pairs.append(((core * RING + z) * RING + y, (core * RING + to[0]) * RING + to[1]))
    return lax.ppermute(value, ("core", "z", "y"), pairs)


def gathered_round(value, half):
    left = shift(value, True, 1)
    right = shift(value, True, -1)
    far_low = shift(left[:half], True, 1)
    far_high = shift(right[half:], True, -1)
    return [value, left, right, far_low, far_high]


def from_others(value):
    return [shift(value, False, by) for by in (2, 1, -1)]


def summed(own, far, left, right):
    return (own + far) + (left + right)


def reward_of(state, goal, action):
    miss = state - goal
    return -jnp.mean(miss * miss, axis=1, keepdims=True) - 0.1 * jnp.mean(action * action, axis=1, keepdims=True)


def change_of(state, action, win_ref, block_refs):
    inputs = jnp.concatenate([state, action], axis=1).astype(jnp.bfloat16)
    pieces = []
    for at in range(win_ref.shape[0]):
        pre = jnp.dot(inputs, win_ref[at], preferred_element_type=jnp.float32)
        pieces.append(silu(pre).astype(jnp.bfloat16))
    hidden_one = jnp.concatenate(pieces, axis=1)
    hidden = hidden_one.shape[1]
    own_ref, left_ref, right_ref, low_ref, high_ref = block_refs
    half = low_ref.shape[0]
    total = jnp.zeros(state.shape, jnp.float32)
    for ref in (own_ref, left_ref, right_ref, high_ref):
        if ref is high_ref:
            depth = hidden - half
            pre = jnp.dot(hidden_one[:, :half], low_ref[...], preferred_element_type=jnp.float32) + jnp.dot(
                hidden_one[:, half:], high_ref[:depth, :], preferred_element_type=jnp.float32
            )
        else:
            depth = hidden
            pre = jnp.dot(hidden_one, ref[:depth, :], preferred_element_type=jnp.float32)
        hidden_two = silu(pre).astype(jnp.bfloat16)
        width = state.shape[1]
        out = jnp.concatenate([ref[depth:, :width], ref[depth:, width:]], axis=0)
        total = total + jnp.dot(hidden_two, out, preferred_element_type=jnp.float32)
    return total


def first_kernel(start_ref, action_ref, win_ref, *refs):
    rows = action_ref.shape[0]
    state = jnp.broadcast_to(start_ref[...], (rows, start_ref.shape[1]))
    refs[-1][...] = change_of(state, action_ref[...], win_ref, refs[:-1])


def step_kernel(
    state_ref, own_ref, far_ref, left_ref, right_ref, reward_ref, before_ref, action_ref, goal_ref, win_ref, *refs
):
    state_out, reward_out, change_out = refs[-3:]
    state = state_ref[...] + summed(own_ref[...], far_ref[...], left_ref[...], right_ref[...])
    state_out[...] = state
    reward_out[...] = reward_ref[...] + reward_of(state, goal_ref[...], before_ref[...])
    change_out[...] = change_of(state, action_ref[...], win_ref, refs[:-3])


def report_kernel(
    row_ref, state_ref, own_ref, far_ref, left_ref, right_ref, reward_ref, before_ref, goal_ref, flags_ref, out_ref
):
    state = state_ref[...] + summed(own_ref[...], far_ref[...], left_ref[...], right_ref[...])
    returns = reward_ref[...] + reward_of(state, goal_ref[...], before_ref[...])
    flags = flags_ref[...]
    rows = returns.shape[0]
    shape = (rows, out_ref.shape[1])
    lane = lax.broadcasted_iota(jnp.int32, shape, 1)
    row = lax.broadcasted_iota(jnp.int32, shape, 0)
    valid = flags[:, 0:1]
    spread = (
        jnp.where(lane == row, valid * returns, 0.0)
        + jnp.where(lane == row + rows, valid, 0.0)
        + jnp.where(lane == row + 2 * rows, flags[:, 1:2], 0.0)
    )
    message = jnp.sum(spread, axis=0, keepdims=True)
    place = lax.broadcasted_iota(jnp.int32, out_ref.shape, 0)
    out_ref[...] = jnp.where(place == row_ref[0], message, 0.0)


def finish(count, at_ref, own_ref, other_ref, actions_ref, dispatch_ref, scores_ref, mean_ref, std_ref):
    message = own_ref[...] + other_ref[...]
    lanes = actions_ref.shape[1]
    returns = message[:, :lanes]
    valid = message[:, lanes : 2 * lanes]
    elite = message[:, 2 * lanes : 3 * lanes]
    return_mean = jnp.sum(returns, keepdims=True) / count
    off = (returns - return_mean) * valid
    return_var = jnp.sum(off * off, keepdims=True) / count
    scores = off / jnp.sqrt(return_var + 1e-06)
    weights = elite * (0.5 + jax.nn.sigmoid(scores))
    groups = scores.shape[0] // CORES
    each = dispatch_ref.shape[0] // groups
    own_core = at_ref[0]
    here = jnp.where(own_core == 0, scores[:groups], scores[groups:])
    lane = lax.broadcasted_iota(jnp.int32, here.shape, 1)
    own = jnp.zeros(scores_ref.shape, jnp.float32)
    for j in range(each):
        column = jnp.sum(jnp.where(lane == at_ref[1] * each + j, here, 0.0), axis=1, keepdims=True)
        own = own + jnp.sum(column * dispatch_ref[j * groups : (j + 1) * groups, :], axis=0, keepdims=True)
    scores_ref[...] = own
    weight_sum = jnp.sum(weights, keepdims=True)
    total = jnp.zeros(actions_ref.shape[2:], jnp.float32)
    for core in range(CORES):
        part = weights[core * groups : (core + 1) * groups]
        for l in range(lanes):
            total = total + part[:, l : l + 1] * actions_ref[core, l]
    mean = jnp.sum(total, axis=0, keepdims=True) / weight_sum
    total = jnp.zeros(actions_ref.shape[2:], jnp.float32)
    for core in range(CORES):
        part = weights[core * groups : (core + 1) * groups]
        for l in range(lanes):
            away = actions_ref[core, l] - mean
            total = total + part[:, l : l + 1] * (away * away)
    var = jnp.sum(total, axis=0, keepdims=True) / weight_sum
    mean_ref[...] = mean
    std_ref[...] = jnp.sqrt(var + 1e-06)


def call(kernel, out_shape, args, smem=0):
    vmem = pl.BlockSpec(memory_space=pltpu.VMEM)
    specs = [pl.BlockSpec(memory_space=pltpu.SMEM)] * smem + [vmem] * (len(args) - smem)
    many = isinstance(out_shape, tuple)
    return pl.pallas_call(
        kernel,
        out_shape=out_shape,
        in_specs=specs,
        out_specs=tuple([vmem] * len(out_shape)) if many else vmem,
        compiler_params=pltpu.CompilerParams(vmem_limit_bytes=48 * 1024 * 1024),
    )(*args)


def on_device(start_state, goal, mean_prev, std_prev, noise, members, elites, w_in, w_hid, w_out):
    local_count = noise.shape[0]
    member_count, hidden, block = w_hid.shape
    width = start_state.shape[0]
    action_width = mean_prev.shape[0] // HORIZON
    plane = lax.axis_index("x")
    core = lax.axis_index("core")
    z, y = lax.axis_index("z"), lax.axis_index("y")
    group = jnp.where(core == 0, y, z)
    each = 16

    own_hid = lax.dynamic_index_in_dim(w_hid, plane, 0, False)
    own_out = lax.dynamic_index_in_dim(w_out, plane, 0, False)
    own_out = jnp.concatenate([own_out[: block // 2], own_out[block // 2 :]], axis=1)
    mine = jnp.concatenate([own_hid, own_out], axis=0)
    blocks = gathered_round(mine, hidden // 2)
    own_in = lax.dynamic_index_in_dim(w_in, plane, 0, True)
    input_layer = lax.all_to_all(
        jnp.broadcast_to(own_in, (RING * RING, *own_in.shape[1:])), ("z", "y"), 0, 0, tiled=True
    )

    actions = mean_prev[None, :] + std_prev[None, :] * noise
    onehot = (members == jnp.arange(member_count, dtype=jnp.int32)[None, :]).astype(jnp.float32)
    before = jnp.cumsum(onehot, axis=0) - onehot
    position = jnp.sum(before * onehot, axis=1).astype(jnp.int32)
    slot = (position % each) * (member_count * RING) + members[:, 0] * RING + position // each
    slot_count = each * member_count * RING
    dispatch = (slot[None, :] == jnp.arange(slot_count, dtype=jnp.int32)[:, None]).astype(jnp.float32)
    first_index = (plane * CORES + core) * local_count
    numbers = first_index + jnp.arange(local_count, dtype=jnp.int32)
    chosen = jnp.sum((elites[:, None] == numbers[None, :]).astype(jnp.float32), axis=0)
    flags = jnp.stack([jnp.ones_like(chosen), chosen], axis=1)
    flags = jnp.concatenate([flags, jnp.zeros((local_count, 126), jnp.float32)], axis=1)
    table = jnp.concatenate([actions, flags], axis=1)
    slot_table = jnp.dot(dispatch, table, precision=lax.Precision.HIGHEST)
    slot_actions = slot_table[:, : actions.shape[1]].reshape(each, member_count * RING, -1)
    all_actions = lax.all_gather(slot_actions, ("core", "x"), axis=0, tiled=True)
    all_actions = all_actions.reshape(CORES, RING * each, member_count * RING, -1)

    to_send = lax.dynamic_index_in_dim(
        slot_table.reshape(each, member_count, RING, -1), group, 2, False
    ).transpose(1, 0, 2)
    rows = lax.all_to_all(to_send, "x", 0, 0, tiled=True).reshape(RING * each, -1)
    row_flags = rows[:, actions.shape[1] :]
    action_of = [rows[:, t * action_width : (t + 1) * action_width] for t in range(HORIZON)]
    row_count = rows.shape[0]

    goal_row = goal[None, :]
    start_row = start_state[None, :]
    tile = jax.ShapeDtypeStruct((row_count, width), jnp.float32)
    column = jax.ShapeDtypeStruct((row_count, 1), jnp.float32)
    state = jnp.broadcast_to(start_row, tile.shape)
    reward = jnp.zeros(column.shape, jnp.float32)
    change = call(first_kernel, tile, (start_row, action_of[0], input_layer, *blocks))
    for t in range(1, HORIZON):
        parts = from_others(change)
        state, reward, change = call(
            step_kernel,
            (tile, column, tile),
            (state, change, *parts, reward, action_of[t - 1], action_of[t], goal_row, input_layer, *blocks),
        )
    parts = from_others(change)
    groups = member_count * RING
    place = (core * groups + plane * RING + group).astype(jnp.int32).reshape(1)
    board = jax.ShapeDtypeStruct((CORES * groups, 4 * row_count), jnp.float32)
    report = call(
        report_kernel,
        board,
        (place, state, change, *parts, reward, action_of[HORIZON - 1], goal_row, row_flags),
        smem=1,
    )
    report = report + sum(shift(report, True, by) for by in (1, 2, 3))
    around = [(i, (i + by) % RING) for by in (1, 2, 3) for i in range(RING)]
    report = report + sum(lax.ppermute(report, "x", around[RING * i : RING * (i + 1)]) for i in range(3))
    other = lax.ppermute(report, "core", [(0, 1), (1, 0)])
    at = jnp.stack([core, plane]).astype(jnp.int32)
    count = float(local_count * CORES * RING)
    line = jax.ShapeDtypeStruct((1, width), jnp.float32)
    scores, new_mean, new_std = call(
        functools.partial(finish, count),
        (jax.ShapeDtypeStruct((1, local_count), jnp.float32), line, line),
        (at, report, other, all_actions, dispatch),
        smem=1,
    )
    return (scores.reshape(local_count), new_mean.reshape(width), new_std.reshape(width))


def solution(mesh):
    chips = Mesh(mesh.devices.reshape(RING, CORES, RING, RING), ("x", "core", "z", "y"))
    cand, tp = ("x", "core"), ("z", "y")
    placed = (
        P(),
        P(),
        P(),
        P(),
        P(cand, None),
        P(cand, None),
        P(),
        P(None, None, tp),
        P(None, None, tp),
        P(None, tp, None),
    )
    return jax.shard_map(
        on_device, mesh=chips, in_specs=placed, out_specs=(P(cand), P(), P()), check_vma=False
    )
```

```python
import functools
import jax
import jax.numpy as jnp
from jax import lax
from jax.experimental import pallas as pl
from jax.experimental.pallas import tpu as pltpu
from jax.sharding import Mesh, PartitionSpec as P

HORIZON = 8
RING = 4
CORES = 2


def silu(v):
    return (0.5 * v) * (1.0 + jnp.tanh(0.5 * v))


def shift(value, own_axis, by):
    pairs = []
    for core in range(CORES):
        for z in range(RING):
            for y in range(RING):
                along_y = (core == 1) == own_axis
                to = (z, (y + by) % RING) if along_y else ((z + by) % RING, y)
                pairs.append(((core * RING + z) * RING + y, (core * RING + to[0]) * RING + to[1]))
    return lax.ppermute(value, ("core", "z", "y"), pairs)


def gathered_round(low, high):
    left_low, right_high = shift(low, True, 1), shift(high, True, -1)
    left_high, right_low = shift(high, True, 1), shift(low, True, -1)
    far_low, far_high = shift(left_low, True, 1), shift(right_high, True, -1)
    return [low, high, left_low, left_high, right_low, right_high, far_low, far_high]


def from_others(value):
    return [shift(value, False, by) for by in (2, 1, -1)]


def summed(own, far, left, right):
    return (own + far) + (left + right)


def reward_of(state, goal, action):
    miss = state - goal
    return -jnp.mean(miss * miss, axis=1, keepdims=True) - 0.1 * jnp.mean(action * action, axis=1, keepdims=True)


def change_of(state, action, win_ref, block_refs, copies=()):
    inputs = jnp.concatenate([state, action], axis=1).astype(jnp.bfloat16)
    pieces = []
    for at in range(win_ref.shape[0]):
        pre = jnp.dot(inputs, win_ref[at], preferred_element_type=jnp.float32)
        pieces.append(silu(pre).astype(jnp.bfloat16))
    hidden_one = jnp.concatenate(pieces, axis=1)
    hidden = hidden_one.shape[1]
    half = block_refs[0].shape[0]
    total = jnp.zeros(state.shape, jnp.float32)
    depth = hidden - half
    for at in range(0, len(block_refs), 2):
        for copy in copies[at : at + 2]:
            copy.wait()
        low_ref, ref = block_refs[at], block_refs[at + 1]
        pre = jnp.dot(hidden_one[:, :half], low_ref[...], preferred_element_type=jnp.float32) + jnp.dot(
            hidden_one[:, half:], ref[:depth, :], preferred_element_type=jnp.float32
        )
        hidden_two = silu(pre).astype(jnp.bfloat16)
        width = state.shape[1]
        out = jnp.concatenate([ref[depth:, :width], ref[depth:, width:]], axis=0)
        total = total + jnp.dot(hidden_two, out, preferred_element_type=jnp.float32)
    return total


def prepare_kernel(ids_ref, hid_ref, out_ref, in_ref, low_ref, high_ref, spread_ref, own_in_ref, sems):
    plane, core = ids_ref[0], ids_ref[1]
    half, block = low_ref.shape
    depth = hid_ref.shape[1] - half
    width = out_ref.shape[2]
    copies = [
        pltpu.make_async_copy(in_ref.at[plane], own_in_ref, sems.at[0]),
        pltpu.make_async_copy(hid_ref.at[plane, pl.ds(0, half), :], low_ref, sems.at[1]),
        pltpu.make_async_copy(hid_ref.at[plane, pl.ds(half, depth), :], high_ref.at[pl.ds(0, depth), :], sems.at[2]),
    ]
    for i in range(block // width):
        copies.append(
            pltpu.make_async_copy(
                out_ref.at[plane, pl.ds(i * width, width), :],
                high_ref.at[pl.ds(depth, width), pl.ds(i * width, width)],
                sems.at[3 + i],
            )
        )
    for copy in copies:
        copy.start()
    copies[0].wait()
    lanes = spread_ref.shape[2]
    own = jnp.where(core == 0, own_in_ref[:, :lanes], own_in_ref[:, lanes:])
    for i in range(spread_ref.shape[0]):
        spread_ref[i] = own
    for copy in copies[1:]:
        copy.wait()


def exact(a, b):
    return jnp.dot(a, b, precision=lax.Precision.HIGHEST, preferred_element_type=jnp.float32)


def dispatch_kernel(
    each, ids_ref, members_ref, elites_ref, noise_ref, mean_ref, std_ref, send_ref, actions_ref, dispatch_ref
):
    plane, core = ids_ref[0], ids_ref[1]
    group = jnp.where(core == 0, ids_ref[2], ids_ref[3])
    count = noise_ref.shape[0]
    member = members_ref[...]
    onehot = jnp.where(lax.broadcasted_iota(jnp.int32, (8, count), 0) == member, 1.0, 0.0)
    earlier = lax.broadcasted_iota(jnp.int32, (count, count), 0) < lax.broadcasted_iota(jnp.int32, (count, count), 1)
    before = jnp.dot(onehot, jnp.where(earlier, 1.0, 0.0), preferred_element_type=jnp.float32)
    position = jnp.sum(before * onehot, axis=0, keepdims=True).astype(jnp.int32)
    part, turn = position // each, position % each
    slot = turn * (RING * RING) + member * RING + part
    dispatch = jnp.where(lax.broadcasted_iota(jnp.int32, dispatch_ref.shape, 0) == slot, 1.0, 0.0)
    dispatch_ref[...] = dispatch
    actions = mean_ref[...] + std_ref[...] * noise_ref[...]
    actions_ref[...] = exact(dispatch, actions)
    away = (member + (RING - plane)) % RING
    near = jnp.where(part == group, away * each + turn, -1)
    picked = jnp.where(lax.broadcasted_iota(jnp.int32, (RING * each, count), 0) == near, 1.0, 0.0)
    width = actions.shape[1]
    send_ref[:, :width] = exact(picked, actions)
    numbers = lax.broadcasted_iota(jnp.int32, (count, elites_ref.shape[1]), 0) + (plane * CORES + core) * count
    chosen = jnp.sum(jnp.where(numbers == elites_ref[...], 1.0, 0.0), axis=1, keepdims=True)
    lane = lax.broadcasted_iota(jnp.int32, (count, width), 1)
    flags = jnp.where(lane == 0, 1.0, jnp.where(lane == 1, chosen, 0.0))
    send_ref[:, width:] = jnp.dot(picked, flags, preferred_element_type=jnp.float32)


def first_kernel(start_ref, own_ref, by_one_ref, by_two_ref, by_three_ref, win_ref, *refs):
    count = (len(refs) - 5) // 2
    sources, (state_out, reward_out, rows_out, change_out), kept = refs[:count], refs[count : count + 4], refs[count + 4 : -1]
    sems = refs[-1]
    copies = [pltpu.make_async_copy(a, b, sems.at[i]) for i, (a, b) in enumerate(zip(sources, kept))]
    for copy in copies:
        copy.start()
    rows = jnp.concatenate([own_ref[...], by_one_ref[...], by_two_ref[...], by_three_ref[...]], axis=0)
    rows_out[...] = rows
    state = jnp.broadcast_to(start_ref[...], state_out.shape)
    state_out[...] = state
    reward_out[...] = jnp.zeros(reward_out.shape, jnp.float32)
    width = win_ref.shape[1] - state.shape[1]
    change_out[...] = change_of(state, rows[:, :width], win_ref, kept, copies)


def step_kernel(t, state_ref, own_ref, far_ref, left_ref, right_ref, reward_ref, rows_ref, goal_ref, win_ref, *refs):
    state_out, reward_out, change_out = refs[-3:]
    state = state_ref[...] + summed(own_ref[...], far_ref[...], left_ref[...], right_ref[...])
    state_out[...] = state
    width = win_ref.shape[1] - state.shape[1]
    before = rows_ref[:, (t - 1) * width : t * width]
    action = rows_ref[:, t * width : (t + 1) * width]
    reward_out[...] = reward_ref[...] + reward_of(state, goal_ref[...], before)
    change_out[...] = change_of(state, action, win_ref, refs[:-3])


def report_kernel(
    action_width, ids_ref, state_ref, own_ref, far_ref, left_ref, right_ref, reward_ref, rows_ref, goal_ref, out_ref
):
    plane, core = ids_ref[0], ids_ref[1]
    group = jnp.where(core == 0, ids_ref[2], ids_ref[3])
    state = state_ref[...] + summed(own_ref[...], far_ref[...], left_ref[...], right_ref[...])
    width = state.shape[1]
    before = rows_ref[:, width - action_width : width]
    returns = reward_ref[...] + reward_of(state, goal_ref[...], before)
    rows = returns.shape[0]
    each = rows // RING
    shape = (rows, out_ref.shape[1])
    lane = lax.broadcasted_iota(jnp.int32, shape, 1)
    row = lax.broadcasted_iota(jnp.int32, shape, 0)
    home = ((plane + RING - row // each) % RING) * each + row % each
    valid = rows_ref[:, width : width + 1]
    spread = (
        jnp.where(lane == home, valid * returns, 0.0)
        + jnp.where(lane == home + rows, valid, 0.0)
        + jnp.where(lane == home + 2 * rows, rows_ref[:, width + 1 : width + 2], 0.0)
    )
    message = jnp.sum(spread, axis=0, keepdims=True)
    place = lax.broadcasted_iota(jnp.int32, out_ref.shape, 0)
    out_ref[...] = jnp.where(place == (core * RING + plane) * RING + group, message, 0.0)


def finish(count, at_ref, own_ref, other_ref, actions_ref, dispatch_ref, scores_ref, mean_ref, std_ref):
    message = own_ref[...] + other_ref[...]
    lanes = actions_ref.shape[1]
    returns = message[:, :lanes]
    valid = message[:, lanes : 2 * lanes]
    elite = message[:, 2 * lanes : 3 * lanes]
    return_mean = jnp.sum(returns, keepdims=True) / count
    off = (returns - return_mean) * valid
    return_var = jnp.sum(off * off, keepdims=True) / count
    scores = off / jnp.sqrt(return_var + 1e-06)
    weights = elite * (0.5 + jax.nn.sigmoid(scores))
    groups = scores.shape[0] // CORES
    each = dispatch_ref.shape[0] // groups
    plane, own_core = at_ref[0], at_ref[1]
    here = jnp.where(own_core == 0, scores[:groups], scores[groups:])
    lane = lax.broadcasted_iota(jnp.int32, here.shape, 1)
    own = jnp.zeros(scores_ref.shape, jnp.float32)
    for j in range(each):
        column = jnp.sum(jnp.where(lane == plane * each + j, here, 0.0), axis=1, keepdims=True)
        own = own + jnp.sum(column * dispatch_ref[j * groups : (j + 1) * groups, :], axis=0, keepdims=True)
    scores_ref[...] = own
    weight_sum = jnp.sum(weights, keepdims=True)
    total = jnp.zeros(actions_ref.shape[2:], jnp.float32)
    for core in range(CORES):
        part = weights[core * groups : (core + 1) * groups]
        for l in range(lanes):
            total = total + part[:, l : l + 1] * actions_ref[core, l]
    mean = jnp.sum(total, axis=0, keepdims=True) / weight_sum
    total = jnp.zeros(actions_ref.shape[2:], jnp.float32)
    for core in range(CORES):
        part = weights[core * groups : (core + 1) * groups]
        for l in range(lanes):
            away = actions_ref[core, l] - mean
            total = total + part[:, l : l + 1] * (away * away)
    var = jnp.sum(total, axis=0, keepdims=True) / weight_sum
    mean_ref[...] = mean
    std_ref[...] = jnp.sqrt(var + 1e-06)


VMEM = pl.BlockSpec(memory_space=pltpu.VMEM)
SMEM = pl.BlockSpec(memory_space=pltpu.SMEM)
ANY = pl.BlockSpec(memory_space=pl.ANY)


def call(kernel, out_shape, args, specs=(), scratch=()):
    specs = list(specs) + [VMEM] * (len(args) - len(specs))
    many = isinstance(out_shape, tuple)
    return pl.pallas_call(
        kernel,
        out_shape=out_shape,
        in_specs=specs,
        out_specs=tuple([VMEM] * len(out_shape)) if many else VMEM,
        scratch_shapes=list(scratch),
        compiler_params=pltpu.CompilerParams(vmem_limit_bytes=16 * 1024 * 1024),
    )(*args)


def on_device(start_state, goal, mean_prev, std_prev, noise, members, elites, w_in, w_hid, w_out):
    local_count = noise.shape[0]
    member_count, hidden, block = w_hid.shape
    width = start_state.shape[0]
    inputs = w_in.shape[1]
    action_width = mean_prev.shape[0] // HORIZON
    each = 16
    ids = jnp.stack([lax.axis_index(name) for name in ("x", "core", "z", "y")]).astype(jnp.int32)
    core = lax.axis_index("core")

    def floats(*shape):
        return jax.ShapeDtypeStruct(shape, jnp.float32)

    def halves(*shape):
        return jax.ShapeDtypeStruct(shape, jnp.bfloat16)

    low, high, spread = call(
        prepare_kernel,
        (
            halves(hidden // 2, block),
            halves(hidden // 2 + width, block),
            halves(RING * RING, inputs, block // 2),
        ),
        (ids, w_hid, w_out, w_in),
        (SMEM, ANY, ANY, ANY),
        (pltpu.VMEM((inputs, block), jnp.bfloat16), pltpu.SemaphoreType.DMA((3 + block // width,))),
    )
    own_half = lax.all_to_all(spread, ("z", "y"), 0, 0, tiled=True)
    other_half = lax.ppermute(own_half, "core", [(0, 1), (1, 0)])
    input_layer = jnp.concatenate(
        [jnp.where(core == 0, own_half, other_half), jnp.where(core == 0, other_half, own_half)], axis=2
    )
    blocks = gathered_round(low, high)

    slot_count = each * member_count * RING
    send, slot_actions, dispatch = call(
        functools.partial(dispatch_kernel, each),
        (floats(RING * each, 2 * width), floats(slot_count, width), floats(slot_count, local_count)),
        (ids, members.reshape(1, local_count), elites[None, :], noise, mean_prev[None, :], std_prev[None, :]),
        (SMEM,),
    )
    all_actions = lax.all_gather(slot_actions.reshape(each, member_count * RING, width), ("core", "x"), axis=0, tiled=True)
    all_actions = all_actions.reshape(CORES, RING * each, member_count * RING, width)
    arrived = [send[:each]]
    for by in range(1, RING):
        arrived.append(lax.ppermute(send[by * each : (by + 1) * each], "x", [(i, (i + by) % RING) for i in range(RING)]))

    goal_row = goal[None, :]
    start_row = start_state[None, :]
    row_count = RING * each
    tile, column = floats(row_count, width), floats(row_count, 1)
    state, reward, rows, change, *blocks = call(
        first_kernel,
        (tile, column, floats(row_count, 2 * width), tile, *(halves(*piece.shape) for piece in blocks)),
        (start_row, *arrived, input_layer, *blocks),
        (VMEM,) * 6 + (ANY,) * len(blocks),
        (pltpu.SemaphoreType.DMA((len(blocks),)),),
    )
    for t in range(1, HORIZON):
        state, reward, change = call(
            functools.partial(step_kernel, t),
            (tile, column, tile),
            (state, change, *from_others(change), reward, rows, goal_row, input_layer, *blocks),
        )
    report = call(
        functools.partial(report_kernel, action_width),
        floats(CORES * member_count * RING, 4 * row_count),
        (ids, state, change, *from_others(change), reward, rows, goal_row),
        (SMEM,),
    )
    report = report + sum(shift(report, True, by) for by in (1, 2, 3))
    report = report + sum(
        lax.ppermute(report, "x", [(i, (i + by) % RING) for i in range(RING)]) for by in range(1, RING)
    )
    other = lax.ppermute(report, "core", [(0, 1), (1, 0)])
    count = float(local_count * CORES * RING)
    scores, new_mean, new_std = call(
        functools.partial(finish, count),
        (floats(1, local_count), floats(1, width), floats(1, width)),
        (ids, report, other, all_actions, dispatch),
        (SMEM,),
    )
    return (scores.reshape(local_count), new_mean.reshape(width), new_std.reshape(width))


def solution(mesh):
    chips = Mesh(mesh.devices.reshape(RING, CORES, RING, RING), ("x", "core", "z", "y"))
    cand, tp = ("x", "core"), ("z", "y")
    placed = (
        P(),
        P(),
        P(),
        P(),
        P(cand, None),
        P(cand, None),
        P(),
        P(None, None, tp),
        P(None, None, tp),
        P(None, tp, None),
    )
    return jax.shard_map(
        on_device, mesh=chips, in_specs=placed, out_specs=(P(cand), P(), P()), check_vma=False
    )
```

```python
import functools
import jax
import jax.numpy as jnp
from jax import lax
from jax.experimental import pallas as pl
from jax.experimental.pallas import tpu as pltpu
from jax.sharding import Mesh, PartitionSpec as P

HORIZON = 8
RING = 4
CORES = 2


def silu(v):
    return (0.5 * v) * (1.0 + jnp.tanh(0.5 * v))


def shift(value, own_axis, by):
    pairs = []
    for core in range(CORES):
        for z in range(RING):
            for y in range(RING):
                along_y = (core == 1) == own_axis
                to = (z, (y + by) % RING) if along_y else ((z + by) % RING, y)
                pairs.append(((core * RING + z) * RING + y, (core * RING + to[0]) * RING + to[1]))
    return lax.ppermute(value, ("core", "z", "y"), pairs)


def gathered_round(low, high):
    left_low, right_high = shift(low, True, 1), shift(high, True, -1)
    left_high, right_low = shift(high, True, 1), shift(low, True, -1)
    far_low, far_high = shift(left_low, True, 1), shift(right_high, True, -1)
    return [low, high, left_low, left_high, right_low, right_high, far_low, far_high]


def from_others(value):
    return [shift(value, False, by) for by in (2, 1, -1)]


def summed(own, far, left, right):
    return (own + far) + (left + right)


def reward_of(state, goal, action):
    miss = state - goal
    return -jnp.mean(miss * miss, axis=1, keepdims=True) - 0.1 * jnp.mean(action * action, axis=1, keepdims=True)


def change_of(state, action, win_ref, block_refs, copies=()):
    inputs = jnp.concatenate([state, action], axis=1).astype(jnp.bfloat16)
    pieces = []
    for at in range(win_ref.shape[0]):
        pre = jnp.dot(inputs, win_ref[at], preferred_element_type=jnp.float32)
        pieces.append(silu(pre).astype(jnp.bfloat16))
    hidden_one = jnp.concatenate(pieces, axis=1)
    hidden = hidden_one.shape[1]
    half = block_refs[0].shape[0]
    total = jnp.zeros(state.shape, jnp.float32)
    depth = hidden - half
    for at in range(0, len(block_refs), 2):
        for copy in copies[at : at + 2]:
            copy.wait()
        low_ref, ref = block_refs[at], block_refs[at + 1]
        pre = jnp.dot(hidden_one[:, :half], low_ref[...], preferred_element_type=jnp.float32) + jnp.dot(
            hidden_one[:, half:], ref[:depth, :], preferred_element_type=jnp.float32
        )
        hidden_two = silu(pre).astype(jnp.bfloat16)
        width = state.shape[1]
        out = jnp.concatenate([ref[depth:, :width], ref[depth:, width:]], axis=0)
        total = total + jnp.dot(hidden_two, out, preferred_element_type=jnp.float32)
    return total


def prepare_kernel(ids_ref, hid_ref, out_ref, low_ref, high_ref, sems):
    plane = ids_ref[0]
    half, block = low_ref.shape
    depth = hid_ref.shape[1] - half
    width = out_ref.shape[2]
    copies = [
        pltpu.make_async_copy(hid_ref.at[plane, pl.ds(0, half), :], low_ref, sems.at[0]),
        pltpu.make_async_copy(hid_ref.at[plane, pl.ds(half, depth), :], high_ref.at[pl.ds(0, depth), :], sems.at[1]),
    ]
    for i in range(block // width):
        copies.append(
            pltpu.make_async_copy(
                out_ref.at[plane, pl.ds(i * width, width), :],
                high_ref.at[pl.ds(depth, width), pl.ds(i * width, width)],
                sems.at[2 + i],
            )
        )
    for copy in copies:
        copy.start()
    for copy in copies:
        copy.wait()


def exact(a, b):
    return jnp.dot(a, b, precision=lax.Precision.HIGHEST, preferred_element_type=jnp.float32)


def dispatch_kernel(
    each,
    ids_ref,
    in_ref,
    members_ref,
    elites_ref,
    noise_ref,
    mean_ref,
    std_ref,
    send_ref,
    actions_ref,
    dispatch_ref,
    spread_ref,
):
    plane, core = ids_ref[0], ids_ref[1]
    lanes = spread_ref.shape[2]
    own = jnp.where(core == 0, in_ref[plane, :, :lanes], in_ref[plane, :, lanes:])
    for i in range(spread_ref.shape[0]):
        spread_ref[i] = own
    group = jnp.where(core == 0, ids_ref[2], ids_ref[3])
    count = noise_ref.shape[0]
    member = members_ref[...]
    onehot = jnp.where(lax.broadcasted_iota(jnp.int32, (8, count), 0) == member, 1.0, 0.0)
    earlier = lax.broadcasted_iota(jnp.int32, (count, count), 0) < lax.broadcasted_iota(jnp.int32, (count, count), 1)
    before = jnp.dot(onehot, jnp.where(earlier, 1.0, 0.0), preferred_element_type=jnp.float32)
    position = jnp.sum(before * onehot, axis=0, keepdims=True).astype(jnp.int32)
    part, turn = position // each, position % each
    slot = turn * (RING * RING) + member * RING + part
    dispatch = jnp.where(lax.broadcasted_iota(jnp.int32, dispatch_ref.shape, 0) == slot, 1.0, 0.0)
    dispatch_ref[...] = dispatch
    actions = mean_ref[...] + std_ref[...] * noise_ref[...]
    actions_ref[...] = exact(dispatch, actions)
    away = (member + (RING - plane)) % RING
    near = jnp.where(part == group, away * each + turn, -1)
    picked = jnp.where(lax.broadcasted_iota(jnp.int32, (RING * each, count), 0) == near, 1.0, 0.0)
    width = actions.shape[1]
    send_ref[:, :width] = exact(picked, actions)
    numbers = lax.broadcasted_iota(jnp.int32, (count, elites_ref.shape[1]), 0) + (plane * CORES + core) * count
    chosen = jnp.sum(jnp.where(numbers == elites_ref[...], 1.0, 0.0), axis=1, keepdims=True)
    lane = lax.broadcasted_iota(jnp.int32, (count, width), 1)
    flags = jnp.where(lane == 0, 1.0, jnp.where(lane == 1, chosen, 0.0))
    send_ref[:, width:] = jnp.dot(picked, flags, preferred_element_type=jnp.float32)


def first_kernel(start_ref, own_ref, by_one_ref, by_two_ref, by_three_ref, win_ref, *refs):
    count = (len(refs) - 5) // 2
    sources, (state_out, reward_out, rows_out, change_out), kept = refs[:count], refs[count : count + 4], refs[count + 4 : -1]
    sems = refs[-1]
    copies = [pltpu.make_async_copy(a, b, sems.at[i]) for i, (a, b) in enumerate(zip(sources, kept))]
    for copy in copies:
        copy.start()
    rows = jnp.concatenate([own_ref[...], by_one_ref[...], by_two_ref[...], by_three_ref[...]], axis=0)
    rows_out[...] = rows
    state = jnp.broadcast_to(start_ref[...], state_out.shape)
    state_out[...] = state
    reward_out[...] = jnp.zeros(reward_out.shape, jnp.float32)
    width = win_ref.shape[1] - state.shape[1]
    change_out[...] = change_of(state, rows[:, :width], win_ref, kept, copies)


def step_kernel(t, state_ref, own_ref, far_ref, left_ref, right_ref, reward_ref, rows_ref, goal_ref, win_ref, *refs):
    state_out, reward_out, change_out = refs[-3:]
    state = state_ref[...] + summed(own_ref[...], far_ref[...], left_ref[...], right_ref[...])
    state_out[...] = state
    width = win_ref.shape[1] - state.shape[1]
    before = rows_ref[:, (t - 1) * width : t * width]
    action = rows_ref[:, t * width : (t + 1) * width]
    reward_out[...] = reward_ref[...] + reward_of(state, goal_ref[...], before)
    change_out[...] = change_of(state, action, win_ref, refs[:-3])


def report_kernel(
    action_width, ids_ref, state_ref, own_ref, far_ref, left_ref, right_ref, reward_ref, rows_ref, goal_ref, out_ref
):
    plane, core = ids_ref[0], ids_ref[1]
    group = jnp.where(core == 0, ids_ref[2], ids_ref[3])
    state = state_ref[...] + summed(own_ref[...], far_ref[...], left_ref[...], right_ref[...])
    width = state.shape[1]
    before = rows_ref[:, width - action_width : width]
    returns = reward_ref[...] + reward_of(state, goal_ref[...], before)
    rows = returns.shape[0]
    each = rows // RING
    shape = (rows, out_ref.shape[1])
    lane = lax.broadcasted_iota(jnp.int32, shape, 1)
    row = lax.broadcasted_iota(jnp.int32, shape, 0)
    home = ((plane + RING - row // each) % RING) * each + row % each
    valid = rows_ref[:, width : width + 1]
    spread = (
        jnp.where(lane == home, valid * returns, 0.0)
        + jnp.where(lane == home + rows, valid, 0.0)
        + jnp.where(lane == home + 2 * rows, rows_ref[:, width + 1 : width + 2], 0.0)
    )
    message = jnp.sum(spread, axis=0, keepdims=True)
    place = lax.broadcasted_iota(jnp.int32, out_ref.shape, 0)
    out_ref[...] = jnp.where(place == (core * RING + plane) * RING + group, message, 0.0)


def finish(count, at_ref, own_ref, other_ref, actions_ref, dispatch_ref, scores_ref, mean_ref, std_ref):
    message = own_ref[...] + other_ref[...]
    lanes = actions_ref.shape[1]
    returns = message[:, :lanes]
    valid = message[:, lanes : 2 * lanes]
    elite = message[:, 2 * lanes : 3 * lanes]
    return_mean = jnp.sum(returns, keepdims=True) / count
    off = (returns - return_mean) * valid
    return_var = jnp.sum(off * off, keepdims=True) / count
    scores = off / jnp.sqrt(return_var + 1e-06)
    weights = elite * (0.5 + jax.nn.sigmoid(scores))
    groups = scores.shape[0] // CORES
    each = dispatch_ref.shape[0] // groups
    plane, own_core = at_ref[0], at_ref[1]
    here = jnp.where(own_core == 0, scores[:groups], scores[groups:])
    lane = lax.broadcasted_iota(jnp.int32, here.shape, 1)
    own = jnp.zeros(scores_ref.shape, jnp.float32)
    for j in range(each):
        column = jnp.sum(jnp.where(lane == plane * each + j, here, 0.0), axis=1, keepdims=True)
        own = own + jnp.sum(column * dispatch_ref[j * groups : (j + 1) * groups, :], axis=0, keepdims=True)
    scores_ref[...] = own
    weight_sum = jnp.sum(weights, keepdims=True)
    total = jnp.zeros(actions_ref.shape[2:], jnp.float32)
    for core in range(CORES):
        part = weights[core * groups : (core + 1) * groups]
        for l in range(lanes):
            total = total + part[:, l : l + 1] * actions_ref[core, l]
    mean = jnp.sum(total, axis=0, keepdims=True) / weight_sum
    total = jnp.zeros(actions_ref.shape[2:], jnp.float32)
    for core in range(CORES):
        part = weights[core * groups : (core + 1) * groups]
        for l in range(lanes):
            away = actions_ref[core, l] - mean
            total = total + part[:, l : l + 1] * (away * away)
    var = jnp.sum(total, axis=0, keepdims=True) / weight_sum
    mean_ref[...] = mean
    std_ref[...] = jnp.sqrt(var + 1e-06)


VMEM = pl.BlockSpec(memory_space=pltpu.VMEM)
SMEM = pl.BlockSpec(memory_space=pltpu.SMEM)
ANY = pl.BlockSpec(memory_space=pl.ANY)
HBM = pl.BlockSpec(memory_space=pltpu.HBM)


def call(kernel, out_shape, args, specs=(), scratch=(), grant=16):
    specs = list(specs) + [VMEM] * (len(args) - len(specs))
    many = isinstance(out_shape, tuple)
    return pl.pallas_call(
        kernel,
        out_shape=out_shape,
        in_specs=specs,
        out_specs=tuple([VMEM] * len(out_shape)) if many else VMEM,
        scratch_shapes=list(scratch),
        compiler_params=pltpu.CompilerParams(vmem_limit_bytes=grant * 1024 * 1024),
    )(*args)


def on_device(start_state, goal, mean_prev, std_prev, noise, members, elites, w_in, w_hid, w_out):
    local_count = noise.shape[0]
    member_count, hidden, block = w_hid.shape
    width = start_state.shape[0]
    inputs = w_in.shape[1]
    action_width = mean_prev.shape[0] // HORIZON
    each = 16
    ids = jnp.stack([lax.axis_index(name) for name in ("x", "core", "z", "y")]).astype(jnp.int32)
    core = lax.axis_index("core")

    def floats(*shape):
        return jax.ShapeDtypeStruct(shape, jnp.float32)

    def halves(*shape):
        return jax.ShapeDtypeStruct(shape, jnp.bfloat16)

    low, high = call(
        prepare_kernel,
        (halves(hidden // 2, block), halves(hidden // 2 + width, block)),
        (ids, w_hid, w_out),
        (SMEM, HBM, HBM),
        (pltpu.SemaphoreType.DMA((2 + block // width,)),),
        57,
    )
    slot_count = each * member_count * RING
    send, slot_actions, dispatch, spread = call(
        functools.partial(dispatch_kernel, each),
        (floats(RING * each, 2 * width), floats(slot_count, width), floats(slot_count, local_count), halves(RING * RING, inputs, block // 2)),
        (ids, w_in, members.reshape(1, local_count), elites[None, :], noise, mean_prev[None, :], std_prev[None, :]),
        (SMEM,),
    )
    all_actions = lax.all_gather(slot_actions.reshape(each, member_count * RING, width), ("core", "x"), axis=0, tiled=True)
    all_actions = all_actions.reshape(CORES, RING * each, member_count * RING, width)
    arrived = [send[:each]]
    for by in range(1, RING):
        arrived.append(lax.ppermute(send[by * each : (by + 1) * each], "x", [(i, (i + by) % RING) for i in range(RING)]))
    blocks = gathered_round(low, high)
    own_half = lax.all_to_all(spread, ("z", "y"), 0, 0, tiled=True)
    other_half = lax.ppermute(own_half, "core", [(0, 1), (1, 0)])
    input_layer = jnp.concatenate(
        [jnp.where(core == 0, own_half, other_half), jnp.where(core == 0, other_half, own_half)], axis=2
    )


    goal_row = goal[None, :]
    start_row = start_state[None, :]
    row_count = RING * each
    tile, column = floats(row_count, width), floats(row_count, 1)
    state, reward, rows, change, *blocks = call(
        first_kernel,
        (tile, column, floats(row_count, 2 * width), tile, *(halves(*piece.shape) for piece in blocks)),
        (start_row, *arrived, input_layer, *blocks),
        (VMEM,) * 6 + (ANY,) * len(blocks),
        (pltpu.SemaphoreType.DMA((len(blocks),)),),
    )
    for t in range(1, HORIZON):
        state, reward, change = call(
            functools.partial(step_kernel, t),
            (tile, column, tile),
            (state, change, *from_others(change), reward, rows, goal_row, input_layer, *blocks),
        )
    report = call(
        functools.partial(report_kernel, action_width),
        floats(CORES * member_count * RING, 4 * row_count),
        (ids, state, change, *from_others(change), reward, rows, goal_row),
        (SMEM,),
    )
    report = report + sum(shift(report, True, by) for by in (1, 2, 3))
    report = report + sum(
        lax.ppermute(report, "x", [(i, (i + by) % RING) for i in range(RING)]) for by in range(1, RING)
    )
    other = lax.ppermute(report, "core", [(0, 1), (1, 0)])
    count = float(local_count * CORES * RING)
    scores, new_mean, new_std = call(
        functools.partial(finish, count),
        (floats(1, local_count), floats(1, width), floats(1, width)),
        (ids, report, other, all_actions, dispatch),
        (SMEM,),
    )
    return (scores.reshape(local_count), new_mean.reshape(width), new_std.reshape(width))


def solution(mesh):
    chips = Mesh(mesh.devices.reshape(RING, CORES, RING, RING), ("x", "core", "z", "y"))
    cand, tp = ("x", "core"), ("z", "y")
    placed = (
        P(),
        P(),
        P(),
        P(),
        P(cand, None),
        P(cand, None),
        P(),
        P(None, None, tp),
        P(None, None, tp),
        P(None, tp, None),
    )
    return jax.shard_map(
        on_device, mesh=chips, in_specs=placed, out_specs=(P(cand), P(), P()), check_vma=False
    )
```

```python
import functools
import jax
import jax.numpy as jnp
from jax import lax
from jax.experimental import pallas as pl
from jax.experimental.pallas import tpu as pltpu
from jax.sharding import Mesh, PartitionSpec as P

HORIZON = 8
RING = 4
CORES = 2


def silu(v):
    return (0.5 * v) * (1.0 + jnp.tanh(0.5 * v))


def shift(value, own_axis, by):
    pairs = []
    for core in range(CORES):
        for z in range(RING):
            for y in range(RING):
                along_y = (core == 1) == own_axis
                to = (z, (y + by) % RING) if along_y else ((z + by) % RING, y)
                pairs.append(((core * RING + z) * RING + y, (core * RING + to[0]) * RING + to[1]))
    return lax.ppermute(value, ("core", "z", "y"), pairs)


def gathered_round(low, high):
    left_low, right_high = shift(low, True, 1), shift(high, True, -1)
    left_high, right_low = shift(high, True, 1), shift(low, True, -1)
    far_low, far_high = shift(left_low, True, 1), shift(right_high, True, -1)
    return [low, high, left_low, left_high, right_low, right_high, far_low, far_high]


def from_others(value):
    return [shift(value, False, by) for by in (2, 1, -1)]


def summed(*parts):
    own, far, left, right = (part.astype(jnp.float32) for part in parts)
    return (own + far) + (left + right)


def reward_of(state, goal, action):
    miss = state - goal
    return -jnp.mean(miss * miss, axis=1, keepdims=True) - 0.1 * jnp.mean(action * action, axis=1, keepdims=True)


def change_of(state, action, win_ref, block_refs, copies=()):
    inputs = jnp.concatenate([state, action], axis=1).astype(jnp.bfloat16)
    pieces = []
    for at in range(win_ref.shape[0]):
        pre = jnp.dot(inputs, win_ref[at], preferred_element_type=jnp.float32)
        pieces.append(silu(pre).astype(jnp.bfloat16))
    hidden_one = jnp.concatenate(pieces, axis=1)
    hidden = hidden_one.shape[1]
    half = block_refs[0].shape[0]
    total = jnp.zeros(state.shape, jnp.float32)
    depth = hidden - half
    for at in range(0, len(block_refs), 2):
        for copy in copies[at : at + 2]:
            copy.wait()
        low_ref, ref = block_refs[at], block_refs[at + 1]
        pre = jnp.dot(hidden_one[:, :half], low_ref[...], preferred_element_type=jnp.float32) + jnp.dot(
            hidden_one[:, half:], ref[:depth, :], preferred_element_type=jnp.float32
        )
        hidden_two = silu(pre).astype(jnp.bfloat16)
        width = state.shape[1]
        out = jnp.concatenate([ref[depth:, :width], ref[depth:, width:]], axis=0)
        total = total + jnp.dot(hidden_two, out, preferred_element_type=jnp.float32)
    return total


def prepare_kernel(ids_ref, hid_ref, out_ref, low_ref, high_ref, sems):
    plane = ids_ref[0]
    half, block = low_ref.shape
    depth = hid_ref.shape[1] - half
    width = out_ref.shape[2]
    copies = [
        pltpu.make_async_copy(hid_ref.at[plane, pl.ds(0, half), :], low_ref, sems.at[0]),
        pltpu.make_async_copy(hid_ref.at[plane, pl.ds(half, depth), :], high_ref.at[pl.ds(0, depth), :], sems.at[1]),
    ]
    for i in range(block // width):
        copies.append(
            pltpu.make_async_copy(
                out_ref.at[plane, pl.ds(i * width, width), :],
                high_ref.at[pl.ds(depth, width), pl.ds(i * width, width)],
                sems.at[2 + i],
            )
        )
    for copy in copies:
        copy.start()
    for copy in copies:
        copy.wait()


def exact(a, b):
    return jnp.dot(a, b, precision=lax.Precision.HIGHEST, preferred_element_type=jnp.float32)


def dispatch_kernel(
    each,
    ids_ref,
    in_ref,
    members_ref,
    elites_ref,
    noise_ref,
    mean_ref,
    std_ref,
    send_ref,
    actions_ref,
    dispatch_ref,
    spread_ref,
):
    plane, core = ids_ref[0], ids_ref[1]
    lanes = spread_ref.shape[2]
    own = jnp.where(core == 0, in_ref[plane, :, :lanes], in_ref[plane, :, lanes:])
    for i in range(spread_ref.shape[0]):
        spread_ref[i] = own
    group = jnp.where(core == 0, ids_ref[2], ids_ref[3])
    count = noise_ref.shape[0]
    member = members_ref[...]
    onehot = jnp.where(lax.broadcasted_iota(jnp.int32, (8, count), 0) == member, 1.0, 0.0)
    earlier = lax.broadcasted_iota(jnp.int32, (count, count), 0) < lax.broadcasted_iota(jnp.int32, (count, count), 1)
    before = jnp.dot(onehot, jnp.where(earlier, 1.0, 0.0), preferred_element_type=jnp.float32)
    position = jnp.sum(before * onehot, axis=0, keepdims=True).astype(jnp.int32)
    part, turn = position // each, position % each
    slot = turn * (RING * RING) + member * RING + part
    dispatch = jnp.where(lax.broadcasted_iota(jnp.int32, dispatch_ref.shape, 0) == slot, 1.0, 0.0)
    dispatch_ref[...] = dispatch
    actions = mean_ref[...] + std_ref[...] * noise_ref[...]
    actions_ref[...] = exact(dispatch, actions)
    away = (member + (RING - plane)) % RING
    near = jnp.where(part == group, away * each + turn, -1)
    picked = jnp.where(lax.broadcasted_iota(jnp.int32, (RING * each, count), 0) == near, 1.0, 0.0)
    width = actions.shape[1]
    send_ref[:, :width] = exact(picked, actions)
    numbers = lax.broadcasted_iota(jnp.int32, (count, elites_ref.shape[1]), 0) + (plane * CORES + core) * count
    chosen = jnp.sum(jnp.where(numbers == elites_ref[...], 1.0, 0.0), axis=1, keepdims=True)
    lane = lax.broadcasted_iota(jnp.int32, (count, width), 1)
    flags = jnp.where(lane == 0, 1.0, jnp.where(lane == 1, chosen, 0.0))
    send_ref[:, width:] = jnp.dot(picked, flags, preferred_element_type=jnp.float32)


def first_kernel(start_ref, own_ref, by_one_ref, by_two_ref, by_three_ref, win_ref, *refs):
    count = (len(refs) - 5) // 2
    sources, (state_out, reward_out, rows_out, change_out), kept = refs[:count], refs[count : count + 4], refs[count + 4 : -1]
    sems = refs[-1]
    copies = [pltpu.make_async_copy(a, b, sems.at[i]) for i, (a, b) in enumerate(zip(sources, kept))]
    for copy in copies:
        copy.start()
    rows = jnp.concatenate([own_ref[...], by_one_ref[...], by_two_ref[...], by_three_ref[...]], axis=0)
    rows_out[...] = rows
    state = jnp.broadcast_to(start_ref[...], state_out.shape)
    state_out[...] = state
    reward_out[...] = jnp.zeros(reward_out.shape, jnp.float32)
    width = win_ref.shape[1] - state.shape[1]
    change_out[...] = change_of(state, rows[:, :width], win_ref, kept, copies).astype(change_out.dtype)


def step_kernel(t, state_ref, own_ref, far_ref, left_ref, right_ref, reward_ref, rows_ref, goal_ref, win_ref, *refs):
    state_out, reward_out, change_out = refs[-3:]
    state = state_ref[...] + summed(own_ref[...], far_ref[...], left_ref[...], right_ref[...])
    state_out[...] = state
    width = win_ref.shape[1] - state.shape[1]
    before = rows_ref[:, (t - 1) * width : t * width]
    action = rows_ref[:, t * width : (t + 1) * width]
    reward_out[...] = reward_ref[...] + reward_of(state, goal_ref[...], before)
    change_out[...] = change_of(state, action, win_ref, refs[:-3]).astype(change_out.dtype)


def report_kernel(
    action_width, ids_ref, state_ref, own_ref, far_ref, left_ref, right_ref, reward_ref, rows_ref, goal_ref, out_ref
):
    plane, core = ids_ref[0], ids_ref[1]
    group = jnp.where(core == 0, ids_ref[2], ids_ref[3])
    state = state_ref[...] + summed(own_ref[...], far_ref[...], left_ref[...], right_ref[...])
    width = state.shape[1]
    before = rows_ref[:, width - action_width : width]
    returns = reward_ref[...] + reward_of(state, goal_ref[...], before)
    rows = returns.shape[0]
    each = rows // RING
    shape = (rows, out_ref.shape[1])
    lane = lax.broadcasted_iota(jnp.int32, shape, 1)
    row = lax.broadcasted_iota(jnp.int32, shape, 0)
    home = ((plane + RING - row // each) % RING) * each + row % each
    valid = rows_ref[:, width : width + 1]
    spread = (
        jnp.where(lane == home, valid * returns, 0.0)
        + jnp.where(lane == home + rows, valid, 0.0)
        + jnp.where(lane == home + 2 * rows, rows_ref[:, width + 1 : width + 2], 0.0)
    )
    message = jnp.sum(spread, axis=0, keepdims=True)
    place = lax.broadcasted_iota(jnp.int32, out_ref.shape, 0)
    out_ref[...] = jnp.where(place == (core * RING + plane) * RING + group, message, 0.0)


def finish(count, at_ref, own_ref, other_ref, actions_ref, dispatch_ref, scores_ref, mean_ref, std_ref):
    message = own_ref[...] + other_ref[...]
    lanes = actions_ref.shape[1]
    returns = message[:, :lanes]
    valid = message[:, lanes : 2 * lanes]
    elite = message[:, 2 * lanes : 3 * lanes]
    return_mean = jnp.sum(returns, keepdims=True) / count
    off = (returns - return_mean) * valid
    return_var = jnp.sum(off * off, keepdims=True) / count
    scores = off / jnp.sqrt(return_var + 1e-06)
    weights = elite * (0.5 + jax.nn.sigmoid(scores))
    groups = scores.shape[0] // CORES
    each = dispatch_ref.shape[0] // groups
    plane, own_core = at_ref[0], at_ref[1]
    here = jnp.where(own_core == 0, scores[:groups], scores[groups:])
    lane = lax.broadcasted_iota(jnp.int32, here.shape, 1)
    own = jnp.zeros(scores_ref.shape, jnp.float32)
    for j in range(each):
        column = jnp.sum(jnp.where(lane == plane * each + j, here, 0.0), axis=1, keepdims=True)
        own = own + jnp.sum(column * dispatch_ref[j * groups : (j + 1) * groups, :], axis=0, keepdims=True)
    scores_ref[...] = own
    weight_sum = jnp.sum(weights, keepdims=True)
    total = jnp.zeros(actions_ref.shape[2:], jnp.float32)
    for core in range(CORES):
        part = weights[core * groups : (core + 1) * groups]
        for l in range(lanes):
            total = total + part[:, l : l + 1] * actions_ref[core, l]
    mean = jnp.sum(total, axis=0, keepdims=True) / weight_sum
    total = jnp.zeros(actions_ref.shape[2:], jnp.float32)
    for core in range(CORES):
        part = weights[core * groups : (core + 1) * groups]
        for l in range(lanes):
            away = actions_ref[core, l] - mean
            total = total + part[:, l : l + 1] * (away * away)
    var = jnp.sum(total, axis=0, keepdims=True) / weight_sum
    mean_ref[...] = mean
    std_ref[...] = jnp.sqrt(var + 1e-06)


VMEM = pl.BlockSpec(memory_space=pltpu.VMEM)
SMEM = pl.BlockSpec(memory_space=pltpu.SMEM)
ANY = pl.BlockSpec(memory_space=pl.ANY)
HBM = pl.BlockSpec(memory_space=pltpu.HBM)


def call(kernel, out_shape, args, specs=(), scratch=(), grant=16):
    specs = list(specs) + [VMEM] * (len(args) - len(specs))
    many = isinstance(out_shape, tuple)
    return pl.pallas_call(
        kernel,
        out_shape=out_shape,
        in_specs=specs,
        out_specs=tuple([VMEM] * len(out_shape)) if many else VMEM,
        scratch_shapes=list(scratch),
        compiler_params=pltpu.CompilerParams(vmem_limit_bytes=grant * 1024 * 1024),
    )(*args)


def on_device(start_state, goal, mean_prev, std_prev, noise, members, elites, w_in, w_hid, w_out):
    local_count = noise.shape[0]
    member_count, hidden, block = w_hid.shape
    width = start_state.shape[0]
    inputs = w_in.shape[1]
    action_width = mean_prev.shape[0] // HORIZON
    each = 16
    ids = jnp.stack([lax.axis_index(name) for name in ("x", "core", "z", "y")]).astype(jnp.int32)
    core = lax.axis_index("core")

    def floats(*shape):
        return jax.ShapeDtypeStruct(shape, jnp.float32)

    def halves(*shape):
        return jax.ShapeDtypeStruct(shape, jnp.bfloat16)

    low, high = call(
        prepare_kernel,
        (halves(hidden // 2, block), halves(hidden // 2 + width, block)),
        (ids, w_hid, w_out),
        (SMEM, HBM, HBM),
        (pltpu.SemaphoreType.DMA((2 + block // width,)),),
        57,
    )
    slot_count = each * member_count * RING
    send, slot_actions, dispatch, spread = call(
        functools.partial(dispatch_kernel, each),
        (floats(RING * each, 2 * width), floats(slot_count, width), floats(slot_count, local_count), halves(RING * RING, inputs, block // 2)),
        (ids, w_in, members.reshape(1, local_count), elites[None, :], noise, mean_prev[None, :], std_prev[None, :]),
        (SMEM,),
    )
    all_actions = lax.all_gather(slot_actions.reshape(each, member_count * RING, width), ("core", "x"), axis=0, tiled=True)
    all_actions = all_actions.reshape(CORES, RING * each, member_count * RING, width)
    arrived = [send[:each]]
    for by in range(1, RING):
        arrived.append(lax.ppermute(send[by * each : (by + 1) * each], "x", [(i, (i + by) % RING) for i in range(RING)]))
    blocks = gathered_round(low, high)
    own_half = lax.all_to_all(spread, ("z", "y"), 0, 0, tiled=True)
    other_half = lax.ppermute(own_half, "core", [(0, 1), (1, 0)])
    input_layer = jnp.concatenate(
        [jnp.where(core == 0, own_half, other_half), jnp.where(core == 0, other_half, own_half)], axis=2
    )


    goal_row = goal[None, :]
    start_row = start_state[None, :]
    row_count = RING * each
    tile, column = floats(row_count, width), floats(row_count, 1)
    part = halves(row_count, width)
    state, reward, rows, change, *blocks = call(
        first_kernel,
        (tile, column, floats(row_count, 2 * width), part, *(halves(*piece.shape) for piece in blocks)),
        (start_row, *arrived, input_layer, *blocks),
        (VMEM,) * 6 + (ANY,) * len(blocks),
        (pltpu.SemaphoreType.DMA((len(blocks),)),),
    )
    for t in range(1, HORIZON):
        state, reward, change = call(
            functools.partial(step_kernel, t),
            (tile, column, part),
            (state, change, *from_others(change), reward, rows, goal_row, input_layer, *blocks),
        )
    report = call(
        functools.partial(report_kernel, action_width),
        floats(CORES * member_count * RING, 4 * row_count),
        (ids, state, change, *from_others(change), reward, rows, goal_row),
        (SMEM,),
    )
    report = report + sum(shift(report, True, by) for by in (1, 2, 3))
    report = report + sum(
        lax.ppermute(report, "x", [(i, (i + by) % RING) for i in range(RING)]) for by in range(1, RING)
    )
    other = lax.ppermute(report, "core", [(0, 1), (1, 0)])
    count = float(local_count * CORES * RING)
    scores, new_mean, new_std = call(
        functools.partial(finish, count),
        (floats(1, local_count), floats(1, width), floats(1, width)),
        (ids, report, other, all_actions, dispatch),
        (SMEM,),
    )
    return (scores.reshape(local_count), new_mean.reshape(width), new_std.reshape(width))


def solution(mesh):
    chips = Mesh(mesh.devices.reshape(RING, CORES, RING, RING), ("x", "core", "z", "y"))
    cand, tp = ("x", "core"), ("z", "y")
    placed = (
        P(),
        P(),
        P(),
        P(),
        P(cand, None),
        P(cand, None),
        P(),
        P(None, None, tp),
        P(None, None, tp),
        P(None, tp, None),
    )
    return jax.shard_map(
        on_device, mesh=chips, in_specs=placed, out_specs=(P(cand), P(), P()), check_vma=False
    )
```

```python
import functools
import jax
import jax.numpy as jnp
from jax import lax
from jax.experimental import pallas as pl
from jax.experimental.pallas import tpu as pltpu
from jax.sharding import Mesh, PartitionSpec as P

HORIZON = 8
RING = 4
CORES = 2


def silu(v):
    return (0.5 * v) * (1.0 + jnp.tanh(0.5 * v))


def shift(value, own_axis, by):
    pairs = []
    for core in range(CORES):
        for z in range(RING):
            for y in range(RING):
                along_y = (core == 1) == own_axis
                to = (z, (y + by) % RING) if along_y else ((z + by) % RING, y)
                pairs.append(((core * RING + z) * RING + y, (core * RING + to[0]) * RING + to[1]))
    return lax.ppermute(value, ("core", "z", "y"), pairs)


def gathered_round(low, high):
    left_low, right_high = shift(low, True, 1), shift(high, True, -1)
    left_high, right_low = shift(high, True, 1), shift(low, True, -1)
    far_low, far_high = shift(left_low, True, 1), shift(right_high, True, -1)
    return [low, high, left_low, left_high, right_low, right_high, far_low, far_high]


def from_others(value):
    return [shift(value, False, by) for by in (2, 1, -1)]


def summed(*parts):
    own, far, left, right = (part.astype(jnp.float32) for part in parts)
    return (own + far) + (left + right)


def reward_of(state, goal, action):
    miss = state - goal
    return -jnp.mean(miss * miss, axis=1, keepdims=True) - 0.1 * jnp.mean(action * action, axis=1, keepdims=True)


def change_of(state, action, win_ref, block_refs, copies=()):
    inputs = jnp.concatenate([state, action], axis=1).astype(jnp.bfloat16)
    pieces = []
    for at in range(win_ref.shape[0]):
        pre = jnp.dot(inputs, win_ref[at], preferred_element_type=jnp.float32)
        pieces.append(silu(pre).astype(jnp.bfloat16))
    hidden_one = jnp.concatenate(pieces, axis=1)
    hidden = hidden_one.shape[1]
    half = block_refs[0].shape[0]
    total = jnp.zeros(state.shape, jnp.float32)
    depth = hidden - half
    for at in range(0, len(block_refs), 2):
        for copy in copies[at : at + 2]:
            copy.wait()
        low_ref, ref = block_refs[at], block_refs[at + 1]
        pre = jnp.dot(hidden_one[:, :half], low_ref[...], preferred_element_type=jnp.float32) + jnp.dot(
            hidden_one[:, half:], ref[:depth, :], preferred_element_type=jnp.float32
        )
        hidden_two = silu(pre).astype(jnp.bfloat16)
        width = state.shape[1]
        out = jnp.concatenate([ref[depth:, :width], ref[depth:, width:]], axis=0)
        total = total + jnp.dot(hidden_two, out, preferred_element_type=jnp.float32)
    return total


def prepare_kernel(ids_ref, hid_ref, out_ref, low_ref, high_ref, sems):
    plane = ids_ref[0]
    half, block = low_ref.shape
    depth = hid_ref.shape[1] - half
    width = out_ref.shape[2]
    copies = [
        pltpu.make_async_copy(hid_ref.at[plane, pl.ds(0, half), :], low_ref, sems.at[0]),
        pltpu.make_async_copy(hid_ref.at[plane, pl.ds(half, depth), :], high_ref.at[pl.ds(0, depth), :], sems.at[1]),
    ]
    for i in range(block // width):
        copies.append(
            pltpu.make_async_copy(
                out_ref.at[plane, pl.ds(i * width, width), :],
                high_ref.at[pl.ds(depth, width), pl.ds(i * width, width)],
                sems.at[2 + i],
            )
        )
    for copy in copies:
        copy.start()
    for copy in copies:
        copy.wait()


def exact(a, b):
    return jnp.dot(a, b, precision=lax.Precision.HIGHEST, preferred_element_type=jnp.float32)


def dispatch_kernel(
    each,
    ids_ref,
    in_ref,
    members_ref,
    elites_ref,
    noise_ref,
    mean_ref,
    std_ref,
    send_ref,
    actions_ref,
    dispatch_ref,
    spread_ref,
):
    plane, core = ids_ref[0], ids_ref[1]
    lanes = spread_ref.shape[2]
    own = jnp.where(core == 0, in_ref[plane, :, :lanes], in_ref[plane, :, lanes:])
    for i in range(spread_ref.shape[0]):
        spread_ref[i] = own
    group = jnp.where(core == 0, ids_ref[2], ids_ref[3])
    count = noise_ref.shape[0]
    member = members_ref[...]
    onehot = jnp.where(lax.broadcasted_iota(jnp.int32, (8, count), 0) == member, 1.0, 0.0)
    earlier = lax.broadcasted_iota(jnp.int32, (count, count), 0) < lax.broadcasted_iota(jnp.int32, (count, count), 1)
    before = jnp.dot(onehot, jnp.where(earlier, 1.0, 0.0), preferred_element_type=jnp.float32)
    position = jnp.sum(before * onehot, axis=0, keepdims=True).astype(jnp.int32)
    part, turn = position // each, position % each
    slot = turn * (RING * RING) + member * RING + part
    dispatch = jnp.where(lax.broadcasted_iota(jnp.int32, dispatch_ref.shape, 0) == slot, 1.0, 0.0)
    dispatch_ref[...] = dispatch
    actions = mean_ref[...] + std_ref[...] * noise_ref[...]
    actions_ref[...] = exact(dispatch, actions)
    away = (member + (RING - plane)) % RING
    near = jnp.where(part == group, away * each + turn, -1)
    picked = jnp.where(lax.broadcasted_iota(jnp.int32, (RING * each, count), 0) == near, 1.0, 0.0)
    width = actions.shape[1]
    send_ref[:, :width] = exact(picked, actions)
    numbers = lax.broadcasted_iota(jnp.int32, (count, elites_ref.shape[1]), 0) + (plane * CORES + core) * count
    chosen = jnp.sum(jnp.where(numbers == elites_ref[...], 1.0, 0.0), axis=1, keepdims=True)
    lane = lax.broadcasted_iota(jnp.int32, (count, width), 1)
    flags = jnp.where(lane == 0, 1.0, jnp.where(lane == 1, chosen, 0.0))
    send_ref[:, width:] = jnp.dot(picked, flags, preferred_element_type=jnp.float32)


def first_kernel(start_ref, own_ref, by_one_ref, by_two_ref, by_three_ref, win_ref, *refs):
    count = (len(refs) - 5) // 2
    sources, (state_out, reward_out, rows_out, change_out), kept = refs[:count], refs[count : count + 4], refs[count + 4 : -1]
    sems = refs[-1]
    copies = [pltpu.make_async_copy(a, b, sems.at[i]) for i, (a, b) in enumerate(zip(sources, kept))]
    for copy in copies:
        copy.start()
    rows = jnp.concatenate([own_ref[...], by_one_ref[...], by_two_ref[...], by_three_ref[...]], axis=0)
    rows_out[...] = rows
    state = jnp.broadcast_to(start_ref[...], state_out.shape)
    state_out[...] = state
    reward_out[...] = jnp.zeros(reward_out.shape, jnp.float32)
    width = win_ref.shape[1] - state.shape[1]
    change_out[...] = change_of(state, rows[:, :width], win_ref, kept, copies).astype(change_out.dtype)


def step_kernel(t, state_ref, own_ref, far_ref, left_ref, right_ref, reward_ref, rows_ref, goal_ref, win_ref, *refs):
    state_out, reward_out, change_out = refs[-3:]
    state = state_ref[...] + summed(own_ref[...], far_ref[...], left_ref[...], right_ref[...])
    state_out[...] = state
    width = win_ref.shape[1] - state.shape[1]
    before = rows_ref[:, (t - 1) * width : t * width]
    action = rows_ref[:, t * width : (t + 1) * width]
    reward_out[...] = reward_ref[...] + reward_of(state, goal_ref[...], before)
    change_out[...] = change_of(state, action, win_ref, refs[:-3]).astype(change_out.dtype)


def report_kernel(
    action_width, ids_ref, state_ref, own_ref, far_ref, left_ref, right_ref, reward_ref, rows_ref, goal_ref, out_ref
):
    plane, core = ids_ref[0], ids_ref[1]
    group = jnp.where(core == 0, ids_ref[2], ids_ref[3])
    state = state_ref[...] + summed(own_ref[...], far_ref[...], left_ref[...], right_ref[...])
    width = state.shape[1]
    before = rows_ref[:, width - action_width : width]
    returns = reward_ref[...] + reward_of(state, goal_ref[...], before)
    rows = returns.shape[0]
    each = rows // RING
    shape = (rows, out_ref.shape[1])
    lane = lax.broadcasted_iota(jnp.int32, shape, 1)
    row = lax.broadcasted_iota(jnp.int32, shape, 0)
    home = ((plane + RING - row // each) % RING) * each + row % each
    valid = rows_ref[:, width : width + 1]
    spread = (
        jnp.where(lane == home, valid * returns, 0.0)
        + jnp.where(lane == home + rows, valid, 0.0)
        + jnp.where(lane == home + 2 * rows, rows_ref[:, width + 1 : width + 2], 0.0)
    )
    message = jnp.sum(spread, axis=0, keepdims=True)
    place = lax.broadcasted_iota(jnp.int32, out_ref.shape, 0)
    out_ref[...] = jnp.where(place == core * RING + group, message, 0.0)


def finish(count, at_ref, *refs):
    boards, (actions_ref, dispatch_ref, scores_ref, mean_ref, std_ref) = refs[:RING], refs[RING:]
    shape = (CORES * actions_ref.shape[2], boards[0].shape[1])
    home = lax.broadcasted_iota(jnp.int32, shape, 0) // RING % RING
    message = jnp.zeros(shape, jnp.float32)
    for by, ref in enumerate(boards):
        wide = jnp.concatenate([ref[core * RING : (core + 1) * RING, :] for core in range(CORES) for _ in range(RING)], axis=0)
        message = jnp.where(home == (at_ref[0] + (RING - by)) % RING, wide, message)
    lanes = actions_ref.shape[1]
    returns = message[:, :lanes]
    valid = message[:, lanes : 2 * lanes]
    elite = message[:, 2 * lanes : 3 * lanes]
    return_mean = jnp.sum(returns, keepdims=True) / count
    off = (returns - return_mean) * valid
    return_var = jnp.sum(off * off, keepdims=True) / count
    scores = off / jnp.sqrt(return_var + 1e-06)
    weights = elite * (0.5 + jax.nn.sigmoid(scores))
    groups = scores.shape[0] // CORES
    each = dispatch_ref.shape[0] // groups
    plane, own_core = at_ref[0], at_ref[1]
    here = jnp.where(own_core == 0, scores[:groups], scores[groups:])
    lane = lax.broadcasted_iota(jnp.int32, here.shape, 1)
    own = jnp.zeros(scores_ref.shape, jnp.float32)
    for j in range(each):
        column = jnp.sum(jnp.where(lane == plane * each + j, here, 0.0), axis=1, keepdims=True)
        own = own + jnp.sum(column * dispatch_ref[j * groups : (j + 1) * groups, :], axis=0, keepdims=True)
    scores_ref[...] = own
    weight_sum = jnp.sum(weights, keepdims=True)
    total = jnp.zeros(actions_ref.shape[2:], jnp.float32)
    for core in range(CORES):
        part = weights[core * groups : (core + 1) * groups]
        for l in range(lanes):
            total = total + part[:, l : l + 1] * actions_ref[core, l]
    mean = jnp.sum(total, axis=0, keepdims=True) / weight_sum
    total = jnp.zeros(actions_ref.shape[2:], jnp.float32)
    for core in range(CORES):
        part = weights[core * groups : (core + 1) * groups]
        for l in range(lanes):
            away = actions_ref[core, l] - mean
            total = total + part[:, l : l + 1] * (away * away)
    var = jnp.sum(total, axis=0, keepdims=True) / weight_sum
    mean_ref[...] = mean
    std_ref[...] = jnp.sqrt(var + 1e-06)


VMEM = pl.BlockSpec(memory_space=pltpu.VMEM)
SMEM = pl.BlockSpec(memory_space=pltpu.SMEM)
ANY = pl.BlockSpec(memory_space=pl.ANY)
HBM = pl.BlockSpec(memory_space=pltpu.HBM)


def call(kernel, out_shape, args, specs=(), scratch=(), grant=16):
    specs = list(specs) + [VMEM] * (len(args) - len(specs))
    many = isinstance(out_shape, tuple)
    return pl.pallas_call(
        kernel,
        out_shape=out_shape,
        in_specs=specs,
        out_specs=tuple([VMEM] * len(out_shape)) if many else VMEM,
        scratch_shapes=list(scratch),
        compiler_params=pltpu.CompilerParams(vmem_limit_bytes=grant * 1024 * 1024),
    )(*args)


def on_device(start_state, goal, mean_prev, std_prev, noise, members, elites, w_in, w_hid, w_out):
    local_count = noise.shape[0]
    member_count, hidden, block = w_hid.shape
    width = start_state.shape[0]
    inputs = w_in.shape[1]
    action_width = mean_prev.shape[0] // HORIZON
    each = 16
    ids = jnp.stack([lax.axis_index(name) for name in ("x", "core", "z", "y")]).astype(jnp.int32)
    core = lax.axis_index("core")

    def floats(*shape):
        return jax.ShapeDtypeStruct(shape, jnp.float32)

    def halves(*shape):
        return jax.ShapeDtypeStruct(shape, jnp.bfloat16)

    low, high = call(
        prepare_kernel,
        (halves(hidden // 2, block), halves(hidden // 2 + width, block)),
        (ids, w_hid, w_out),
        (SMEM, HBM, HBM),
        (pltpu.SemaphoreType.DMA((2 + block // width,)),),
        57,
    )
    slot_count = each * member_count * RING
    send, slot_actions, dispatch, spread = call(
        functools.partial(dispatch_kernel, each),
        (floats(RING * each, 2 * width), floats(slot_count, width), floats(slot_count, local_count), halves(RING * RING, inputs, block // 2)),
        (ids, w_in, members.reshape(1, local_count), elites[None, :], noise, mean_prev[None, :], std_prev[None, :]),
        (SMEM,),
    )
    all_actions = lax.all_gather(slot_actions.reshape(each, member_count * RING, width), ("core", "x"), axis=0, tiled=True)
    all_actions = all_actions.reshape(CORES, RING * each, member_count * RING, width)
    arrived = [send[:each]]
    for by in range(1, RING):
        arrived.append(lax.ppermute(send[by * each : (by + 1) * each], "x", [(i, (i + by) % RING) for i in range(RING)]))
    blocks = gathered_round(low, high)
    own_half = lax.all_to_all(spread, ("z", "y"), 0, 0, tiled=True)
    other_half = lax.ppermute(own_half, "core", [(0, 1), (1, 0)])
    input_layer = jnp.concatenate(
        [jnp.where(core == 0, own_half, other_half), jnp.where(core == 0, other_half, own_half)], axis=2
    )


    goal_row = goal[None, :]
    start_row = start_state[None, :]
    row_count = RING * each
    tile, column = floats(row_count, width), floats(row_count, 1)
    part = halves(row_count, width)
    state, reward, rows, change, *blocks = call(
        first_kernel,
        (tile, column, floats(row_count, 2 * width), part, *(halves(*piece.shape) for piece in blocks)),
        (start_row, *arrived, input_layer, *blocks),
        (VMEM,) * 6 + (ANY,) * len(blocks),
        (pltpu.SemaphoreType.DMA((len(blocks),)),),
    )
    for t in range(1, HORIZON):
        state, reward, change = call(
            functools.partial(step_kernel, t),
            (tile, column, part),
            (state, change, *from_others(change), reward, rows, goal_row, input_layer, *blocks),
        )
    report = call(
        functools.partial(report_kernel, action_width),
        floats(CORES * RING, 4 * row_count),
        (ids, state, change, *from_others(change), reward, rows, goal_row),
        (SMEM,),
    )
    report = report + sum(shift(report, True, by) for by in (1, 2, 3))
    report = report + lax.ppermute(report, "core", [(0, 1), (1, 0)])
    boards = [report]
    for by in range(1, RING):
        boards.append(lax.ppermute(report, "x", [(i, (i + by) % RING) for i in range(RING)]))
    count = float(local_count * CORES * RING)
    scores, new_mean, new_std = call(
        functools.partial(finish, count),
        (floats(1, local_count), floats(1, width), floats(1, width)),
        (ids, *boards, all_actions, dispatch),
        (SMEM,),
    )
    return (scores.reshape(local_count), new_mean.reshape(width), new_std.reshape(width))


def solution(mesh):
    chips = Mesh(mesh.devices.reshape(RING, CORES, RING, RING), ("x", "core", "z", "y"))
    cand, tp = ("x", "core"), ("z", "y")
    placed = (
        P(),
        P(),
        P(),
        P(),
        P(cand, None),
        P(cand, None),
        P(),
        P(None, None, tp),
        P(None, None, tp),
        P(None, tp, None),
    )
    return jax.shard_map(
        on_device, mesh=chips, in_specs=placed, out_specs=(P(cand), P(), P()), check_vma=False
    )
```

```python
import functools
import jax
import jax.numpy as jnp
from jax import lax
from jax.experimental import pallas as pl
from jax.experimental.pallas import tpu as pltpu
from jax.sharding import Mesh, PartitionSpec as P

HORIZON = 8
RING = 4
CORES = 2


def silu(v):
    return (0.5 * v) * (1.0 + jnp.tanh(0.5 * v))


def shift(value, own_axis, by):
    pairs = []
    for core in range(CORES):
        for z in range(RING):
            for y in range(RING):
                along_y = (core == 1) == own_axis
                to = (z, (y + by) % RING) if along_y else ((z + by) % RING, y)
                pairs.append(((core * RING + z) * RING + y, (core * RING + to[0]) * RING + to[1]))
    return lax.ppermute(value, ("core", "z", "y"), pairs)


def gathered_round(low, high):
    left_low, right_high = shift(low, True, 1), shift(high, True, -1)
    left_high, right_low = shift(high, True, 1), shift(low, True, -1)
    far_low, far_high = shift(left_low, True, 1), shift(right_high, True, -1)
    return [low, high, left_low, left_high, right_low, right_high, far_low, far_high]


def from_others(value):
    return [shift(value, False, by) for by in (2, 1, -1)]


def summed(*parts):
    own, far, left, right = (part.astype(jnp.float32) for part in parts)
    return (own + far) + (left + right)


def reward_of(state, goal, action):
    miss = state - goal
    return -jnp.mean(miss * miss, axis=1, keepdims=True) - 0.1 * jnp.mean(action * action, axis=1, keepdims=True)


def change_of(state, action, win_ref, block_refs, copies=()):
    inputs = jnp.concatenate([state, action], axis=1).astype(jnp.bfloat16)
    pieces = []
    for at in range(win_ref.shape[0]):
        pre = jnp.dot(inputs, win_ref[at], preferred_element_type=jnp.float32)
        pieces.append(silu(pre).astype(jnp.bfloat16))
    hidden_one = jnp.concatenate(pieces, axis=1)
    hidden = hidden_one.shape[1]
    half = block_refs[0].shape[0]
    total = jnp.zeros(state.shape, jnp.float32)
    depth = hidden - half
    for at in range(0, len(block_refs), 2):
        for copy in copies[at : at + 2]:
            copy.wait()
        low_ref, ref = block_refs[at], block_refs[at + 1]
        pre = jnp.dot(hidden_one[:, :half], low_ref[...], preferred_element_type=jnp.float32) + jnp.dot(
            hidden_one[:, half:], ref[:depth, :], preferred_element_type=jnp.float32
        )
        hidden_two = silu(pre).astype(jnp.bfloat16)
        width = state.shape[1]
        out = jnp.concatenate([ref[depth:, :width], ref[depth:, width:]], axis=0)
        total = total + jnp.dot(hidden_two, out, preferred_element_type=jnp.float32)
    return total


def prepare_kernel(ids_ref, hid_ref, out_ref, low_ref, high_ref, sems):
    plane = ids_ref[0]
    half, block = low_ref.shape
    depth = hid_ref.shape[1] - half
    width = out_ref.shape[2]
    copies = [
        pltpu.make_async_copy(hid_ref.at[plane, pl.ds(0, half), :], low_ref, sems.at[0]),
        pltpu.make_async_copy(hid_ref.at[plane, pl.ds(half, depth), :], high_ref.at[pl.ds(0, depth), :], sems.at[1]),
    ]
    for i in range(block // width):
        copies.append(
            pltpu.make_async_copy(
                out_ref.at[plane, pl.ds(i * width, width), :],
                high_ref.at[pl.ds(depth, width), pl.ds(i * width, width)],
                sems.at[2 + i],
            )
        )
    for copy in copies:
        copy.start()
    for copy in copies:
        copy.wait()


def exact(a, b):
    return jnp.dot(a, b, precision=lax.Precision.HIGHEST, preferred_element_type=jnp.float32)


def dispatch_kernel(
    each,
    ids_ref,
    in_ref,
    members_ref,
    elites_ref,
    noise_ref,
    mean_ref,
    std_ref,
    send_ref,
    actions_ref,
    dispatch_ref,
    spread_ref,
):
    plane, core = ids_ref[0], ids_ref[1]
    lanes = spread_ref.shape[2]
    own = jnp.where(core == 0, in_ref[plane, :, :lanes], in_ref[plane, :, lanes:])
    for i in range(spread_ref.shape[0]):
        spread_ref[i] = own
    group = jnp.where(core == 0, ids_ref[2], ids_ref[3])
    count = noise_ref.shape[0]
    member = members_ref[...]
    onehot = jnp.where(lax.broadcasted_iota(jnp.int32, (8, count), 0) == member, 1.0, 0.0)
    earlier = lax.broadcasted_iota(jnp.int32, (count, count), 0) < lax.broadcasted_iota(jnp.int32, (count, count), 1)
    before = jnp.dot(onehot, jnp.where(earlier, 1.0, 0.0), preferred_element_type=jnp.float32)
    position = jnp.sum(before * onehot, axis=0, keepdims=True).astype(jnp.int32)
    part, turn = position // each, position % each
    slot = turn * (RING * RING) + member * RING + part
    dispatch = jnp.where(lax.broadcasted_iota(jnp.int32, dispatch_ref.shape, 0) == slot, 1.0, 0.0)
    dispatch_ref[...] = dispatch
    actions = mean_ref[...] + std_ref[...] * noise_ref[...]
    actions_ref[...] = exact(dispatch, actions)
    away = (member + (RING - plane)) % RING
    near = jnp.where(part == group, away * each + turn, -1)
    picked = jnp.where(lax.broadcasted_iota(jnp.int32, (RING * each, count), 0) == near, 1.0, 0.0)
    width = actions.shape[1]
    send_ref[:, :width] = exact(picked, actions)
    numbers = lax.broadcasted_iota(jnp.int32, (count, elites_ref.shape[1]), 0) + (plane * CORES + core) * count
    chosen = jnp.sum(jnp.where(numbers == elites_ref[...], 1.0, 0.0), axis=1, keepdims=True)
    lane = lax.broadcasted_iota(jnp.int32, (count, width), 1)
    flags = jnp.where(lane == 0, 1.0, jnp.where(lane == 1, chosen, 0.0))
    send_ref[:, width:] = jnp.dot(picked, flags, preferred_element_type=jnp.float32)


def first_kernel(start_ref, own_ref, by_one_ref, by_two_ref, by_three_ref, win_ref, *refs):
    count = (len(refs) - 5) // 2
    sources, (state_out, reward_out, rows_out, change_out), kept = refs[:count], refs[count : count + 4], refs[count + 4 : -1]
    sems = refs[-1]
    copies = [pltpu.make_async_copy(a, b, sems.at[i]) for i, (a, b) in enumerate(zip(sources, kept))]
    for copy in copies:
        copy.start()
    rows = jnp.concatenate([own_ref[...], by_one_ref[...], by_two_ref[...], by_three_ref[...]], axis=0)
    rows_out[...] = rows
    state = jnp.broadcast_to(start_ref[...], state_out.shape)
    state_out[...] = state
    reward_out[...] = jnp.zeros(reward_out.shape, jnp.float32)
    width = win_ref.shape[1] - state.shape[1]
    change_out[...] = change_of(state, rows[:, :width], win_ref, kept, copies).astype(change_out.dtype)


def step_kernel(t, state_ref, own_ref, far_ref, left_ref, right_ref, reward_ref, rows_ref, goal_ref, win_ref, *refs):
    state_out, reward_out, change_out = refs[-3:]
    state = state_ref[...] + summed(own_ref[...], far_ref[...], left_ref[...], right_ref[...])
    state_out[...] = state
    width = win_ref.shape[1] - state.shape[1]
    before = rows_ref[:, (t - 1) * width : t * width]
    action = rows_ref[:, t * width : (t + 1) * width]
    reward_out[...] = reward_ref[...] + reward_of(state, goal_ref[...], before)
    change_out[...] = change_of(state, action, win_ref, refs[:-3]).astype(change_out.dtype)


def report_kernel(
    action_width, ids_ref, state_ref, own_ref, far_ref, left_ref, right_ref, reward_ref, rows_ref, goal_ref, out_ref
):
    plane, core = ids_ref[0], ids_ref[1]
    group = jnp.where(core == 0, ids_ref[2], ids_ref[3])
    state = state_ref[...] + summed(own_ref[...], far_ref[...], left_ref[...], right_ref[...])
    width = state.shape[1]
    before = rows_ref[:, width - action_width : width]
    returns = reward_ref[...] + reward_of(state, goal_ref[...], before)
    rows = returns.shape[0]
    each = rows // RING
    shape = (rows, out_ref.shape[1])
    lane = lax.broadcasted_iota(jnp.int32, shape, 1)
    row = lax.broadcasted_iota(jnp.int32, shape, 0)
    home = ((plane + RING - row // each) % RING) * each + row % each
    valid = rows_ref[:, width : width + 1]
    spread = (
        jnp.where(lane == home, valid * returns, 0.0)
        + jnp.where(lane == home + rows, valid, 0.0)
        + jnp.where(lane == home + 2 * rows, rows_ref[:, width + 1 : width + 2], 0.0)
    )
    message = jnp.sum(spread, axis=0, keepdims=True)
    place = lax.broadcasted_iota(jnp.int32, out_ref.shape, 0)
    out_ref[...] = jnp.where(place == core * RING + group, message, 0.0)


def finish(count, at_ref, *refs):
    boards, (actions_ref, dispatch_ref, scores_ref, mean_ref, std_ref) = refs[:RING], refs[RING:]
    shape = (CORES * actions_ref.shape[2], boards[0].shape[1])
    home = lax.broadcasted_iota(jnp.int32, shape, 0) // RING % RING
    message = jnp.zeros(shape, jnp.float32)
    for by, ref in enumerate(boards):
        wide = jnp.concatenate([ref[core * RING : (core + 1) * RING, :] for core in range(CORES) for _ in range(RING)], axis=0)
        message = jnp.where(home == (at_ref[0] + (RING - by)) % RING, wide, message)
    lanes = actions_ref.shape[1]
    returns = message[:, :lanes]
    valid = message[:, lanes : 2 * lanes]
    elite = message[:, 2 * lanes : 3 * lanes]
    return_mean = jnp.sum(returns, keepdims=True) / count
    off = (returns - return_mean) * valid
    return_var = jnp.sum(off * off, keepdims=True) / count
    scores = off / jnp.sqrt(return_var + 1e-06)
    weights = elite * (0.5 + jax.nn.sigmoid(scores))
    groups = scores.shape[0] // CORES
    each = dispatch_ref.shape[0] // groups
    plane, own_core = at_ref[0], at_ref[1]
    here = jnp.where(own_core == 0, scores[:groups], scores[groups:])
    lane = lax.broadcasted_iota(jnp.int32, here.shape, 1)
    own = jnp.zeros(scores_ref.shape, jnp.float32)
    for j in range(each):
        column = jnp.sum(jnp.where(lane == plane * each + j, here, 0.0), axis=1, keepdims=True)
        own = own + jnp.sum(column * dispatch_ref[j * groups : (j + 1) * groups, :], axis=0, keepdims=True)
    scores_ref[...] = own
    weight_sum = jnp.sum(weights, keepdims=True)
    total = jnp.zeros(actions_ref.shape[2:], jnp.float32)
    for core in range(CORES):
        part = weights[core * groups : (core + 1) * groups]
        for l in range(lanes):
            total = total + part[:, l : l + 1] * actions_ref[core, l]
    mean = jnp.sum(total, axis=0, keepdims=True) / weight_sum
    total = jnp.zeros(actions_ref.shape[2:], jnp.float32)
    for core in range(CORES):
        part = weights[core * groups : (core + 1) * groups]
        for l in range(lanes):
            away = actions_ref[core, l] - mean
            total = total + part[:, l : l + 1] * (away * away)
    var = jnp.sum(total, axis=0, keepdims=True) / weight_sum
    mean_ref[...] = mean
    std_ref[...] = jnp.sqrt(var + 1e-06)


VMEM = pl.BlockSpec(memory_space=pltpu.VMEM)
SMEM = pl.BlockSpec(memory_space=pltpu.SMEM)
ANY = pl.BlockSpec(memory_space=pl.ANY)
HBM = pl.BlockSpec(memory_space=pltpu.HBM)


def call(kernel, out_shape, args, specs=(), scratch=(), grant=16):
    specs = list(specs) + [VMEM] * (len(args) - len(specs))
    many = isinstance(out_shape, tuple)
    return pl.pallas_call(
        kernel,
        out_shape=out_shape,
        in_specs=specs,
        out_specs=tuple([VMEM] * len(out_shape)) if many else VMEM,
        scratch_shapes=list(scratch),
        compiler_params=pltpu.CompilerParams(vmem_limit_bytes=grant * 1024 * 1024),
    )(*args)


def on_device(start_state, goal, mean_prev, std_prev, noise, members, elites, w_in, w_hid, w_out):
    local_count = noise.shape[0]
    member_count, hidden, block = w_hid.shape
    width = start_state.shape[0]
    inputs = w_in.shape[1]
    action_width = mean_prev.shape[0] // HORIZON
    each = 16
    ids = jnp.stack([lax.axis_index(name) for name in ("x", "core", "z", "y")]).astype(jnp.int32)
    core = lax.axis_index("core")

    def floats(*shape):
        return jax.ShapeDtypeStruct(shape, jnp.float32)

    def halves(*shape):
        return jax.ShapeDtypeStruct(shape, jnp.bfloat16)

    low, high = call(
        prepare_kernel,
        (halves(hidden // 2, block), halves(hidden // 2 + width, block)),
        (ids, w_hid, w_out),
        (SMEM, HBM, HBM),
        (pltpu.SemaphoreType.DMA((2 + block // width,)),),
        57,
    )
    slot_count = each * member_count * RING
    send, slot_actions, dispatch, spread = call(
        functools.partial(dispatch_kernel, each),
        (floats(RING * each, 2 * width), floats(slot_count, width), floats(slot_count, local_count), halves(RING * RING, inputs, block // 2)),
        (ids, w_in, members.reshape(1, local_count), elites[None, :], noise, mean_prev[None, :], std_prev[None, :]),
        (SMEM,),
    )
    all_actions = lax.all_gather(slot_actions.reshape(each, member_count * RING, width), ("core", "x"), axis=0, tiled=True)
    all_actions = all_actions.reshape(CORES, RING * each, member_count * RING, width)
    arrived = [send[:each]]
    for by in range(1, RING):
        arrived.append(lax.ppermute(send[by * each : (by + 1) * each], "x", [(i, (i + by) % RING) for i in range(RING)]))
    blocks = gathered_round(low, high)
    own_half = lax.all_to_all(spread, ("z", "y"), 0, 0, tiled=True)
    other_half = lax.ppermute(own_half, "core", [(0, 1), (1, 0)])
    input_layer = jnp.concatenate(
        [jnp.where(core == 0, own_half, other_half), jnp.where(core == 0, other_half, own_half)], axis=2
    )


    goal_row = goal[None, :]
    start_row = start_state[None, :]
    row_count = RING * each
    tile, column = floats(row_count, width), floats(row_count, 1)
    part = halves(row_count, width)
    state, reward, rows, change, *blocks = call(
        first_kernel,
        (tile, column, floats(row_count, 2 * width), part, *(halves(*piece.shape) for piece in blocks)),
        (start_row, *arrived, input_layer, *blocks),
        (VMEM,) * 6 + (ANY,) * len(blocks),
        (pltpu.SemaphoreType.DMA((len(blocks),)),),
    )
    for t in range(1, HORIZON):
        state, reward, change = call(
            functools.partial(step_kernel, t),
            (tile, column, part),
            (state, change, *from_others(change), reward, rows, goal_row, input_layer, *blocks),
        )
    report = call(
        functools.partial(report_kernel, action_width),
        floats(CORES * RING, 4 * row_count),
        (ids, state, change, *from_others(change), reward, rows, goal_row),
        (SMEM,),
    )
    report, all_actions = lax.optimization_barrier((report, all_actions))
    report = report + sum(shift(report, True, by) for by in (1, 2, 3))
    report = report + lax.ppermute(report, "core", [(0, 1), (1, 0)])
    boards = [report]
    for by in range(1, RING):
        boards.append(lax.ppermute(report, "x", [(i, (i + by) % RING) for i in range(RING)]))
    count = float(local_count * CORES * RING)
    scores, new_mean, new_std = call(
        functools.partial(finish, count),
        (floats(1, local_count), floats(1, width), floats(1, width)),
        (ids, *boards, all_actions, dispatch),
        (SMEM,),
    )
    return (scores.reshape(local_count), new_mean.reshape(width), new_std.reshape(width))


def solution(mesh):
    chips = Mesh(mesh.devices.reshape(RING, CORES, RING, RING), ("x", "core", "z", "y"))
    cand, tp = ("x", "core"), ("z", "y")
    placed = (
        P(),
        P(),
        P(),
        P(),
        P(cand, None),
        P(cand, None),
        P(),
        P(None, None, tp),
        P(None, None, tp),
        P(None, tp, None),
    )
    return jax.shard_map(
        on_device, mesh=chips, in_specs=placed, out_specs=(P(cand), P(), P()), check_vma=False
    )
```
